512 devices in a mesh: ctx: 64 (over z, y_lo, x), seq: 8 (over y_hi, core).
Axes of the slice: x: 4, y: 8 (y_hi: 4, y_lo: 2; y = y_hi * 2 + y_lo), z: 8, core: 2. Of those that a mesh axis runs over, the one named last changes fastest.
Arguments:
- queries: bfloat16 [65536, 4096], P(('seq', 'ctx')), parts along dimension 0, may hold values from -140 to 140
- keys: bfloat16 [65536, 512], P(('seq', 'ctx')), parts along dimension 0, may hold values from -7 to 7
- values: bfloat16 [65536, 512], P(('seq', 'ctx')), parts along dimension 0, may hold values from -6 to 6
- key_value_scales: float32 [2048, 2, 4], P('seq'), parts along dimension 0, may hold values from 0.5 to 2
- doc_lengths: int32 [256], P('seq'), parts along dimension 0, may hold values from 1 to 512, 8192 in all
Outputs:
- attended: bfloat16 [65536, 4096], P(('seq', 'ctx')), parts along dimension 0
The draws below stay inside these ranges and needn't reach their ends.
There are 8 independent parts, one for each index of `seq`. The reference program is written for one: setup_inputs(seed, part) draws one part's arguments, and reference() takes and returns one part's arrays. A program takes and returns all parts, laid end to end along the dimension named above; each array names one. Nothing has to cross between parts.
Inputs may be any that keep to these rules, and one draw needn't show every extreme that they name: doc_lengths sum to 8192; each is at most 512.
All inputs are finite; a program needn't handle non-finite values.
Results may differ from the reference program's by a relative error of at most 0.0047.
Values may be sent and summed in bfloat16 or wider, within the bound.
No kernel may reach another device: no remote copies, remote signals or barrier semaphores. Data moves between devices by JAX's collectives and lax.ppermute only.
A program may use at most 64 MiB of HBM per device.

```python
import math
import jax
import jax.numpy as jnp
import numpy as np
from jax import lax

QUERY_HEADS = 32
KEY_VALUE_HEADS = 4
HEAD_SIZE = 128
TOKENS_PER_SHARD = 128
SCALE_BLOCK = 32
TRACE_TOKENS = 8192
DOC_MOST = 512
DOCS = 32


def shared_keys(key):
    return jnp.clip(jax.random.normal(key, (TRACE_TOKENS, KEY_VALUE_HEADS * HEAD_SIZE), jnp.float32), -6.0, 6.0)


def draw_keys(key, part):
    base_offset = shared_keys(key)
    return base_offset.astype(jnp.bfloat16)


def draw_queries(key, part):
    key = jax.random.fold_in(key, 7)
    fresh = jnp.clip(jax.random.normal(key, (TRACE_TOKENS, QUERY_HEADS * HEAD_SIZE), jnp.float32), -6.0, 6.0)
    return fresh.astype(jnp.bfloat16)


def block_levels(stream_key, shape, shards, least, high):
    gain, own = 1.0, jax.random.fold_in(stream_key, 6)
    for position, shards_of in shards:
        steps = jnp.exp(jax.random.uniform(jax.random.fold_in(own, position), (shards_of,), jnp.float32, least / len(shards), high / len(shards)))
        gain = gain * jnp.repeat(steps, shape[position] // shards_of).reshape([-1 if axis == position else 1 for axis in range(len(shape))])
    return gain


def split_up(amount, total, reach, lean):
    portions = [(1 << 20) // math.isqrt(rank ** lean) + 1 for rank in range(2, amount + 1)]
    surplus, given = total - reach - (amount - 1), [1] * (amount - 1)
    while surplus > 0:
        free = [i for i in range(amount - 1) if given[i] < reach]
        mass, budget = sum([portions[i] for i in free]), surplus
        for i in free:
            extra = min(reach - given[i], max(1, budget * portions[i] // mass), surplus)
            given[i] = given[i] + extra
            surplus = surplus - extra
    return np.array([reach] + given)


def ragged_sizes(stream_key, amount, total, bound, skew):
    if amount == 2:
        one = jax.random.randint(stream_key, (), max(1, total - bound), min(bound, total - 1) + 1)
        return jnp.stack([one, total - one])
    tallies = jnp.asarray(split_up(amount, total, bound, skew), jnp.int32)
    couples = (amount - 1) // 2
    donor, receiver = tallies[1:1 + 2 * couples:2], tallies[2:2 + 2 * couples:2]
    room = jnp.minimum(donor - 1, bound - receiver)
    moved = jax.random.randint(jax.random.fold_in(stream_key, 1), (couples,), 0, 1 << 20) % (room + 1)
    tallies = tallies.at[1:1 + 2 * couples:2].set(donor - moved).at[2:2 + 2 * couples:2].set(receiver + moved)
    return tallies[jax.random.permutation(jax.random.fold_in(stream_key, 2), amount)]


def centred(stream_key, shape, width, most, pieces=(), held_as=jnp.bfloat16):
    loudness = block_levels(stream_key, shape, pieces, -0.22, 0.18) if pieces else 1.0
    array = jax.random.normal(stream_key, shape, jnp.float32) * width * loudness
    return jnp.minimum(jnp.maximum(array, -most), most).astype(held_as)


def setup_inputs(seed: int = 0, part: int = 0) -> dict:
    arg_keys = jax.random.split(jax.random.key(seed), 6)
    own_keys = jax.random.split(jax.random.fold_in(arg_keys[5], part), 6)
    queries = draw_queries(jax.random.fold_in(jax.random.fold_in(arg_keys[5], part), 71), part)
    keys = draw_keys(jax.random.fold_in(jax.random.fold_in(arg_keys[5], part), 71), part)
    values = centred(own_keys[2], (TRACE_TOKENS, KEY_VALUE_HEADS * HEAD_SIZE), 1.0, 6.0, ((0, 64),))
    key_value_scales = jnp.clip(jnp.exp(jax.random.uniform(own_keys[3], (TRACE_TOKENS // SCALE_BLOCK, 2, KEY_VALUE_HEADS), jnp.float32, math.log(0.5), math.log(2.0))), 0.5, 2.0)
    doc_lengths = ragged_sizes(own_keys[4], DOCS, TRACE_TOKENS, DOC_MOST, 2).astype(jnp.int32)
    return dict(queries=queries, keys=keys, values=values, key_value_scales=key_value_scales, doc_lengths=doc_lengths)


def reference(queries, keys, values, key_value_scales, doc_lengths):
    query_group = QUERY_HEADS // KEY_VALUE_HEADS
    pos = jnp.arange(TRACE_TOKENS, dtype=jnp.int32)
    ends = jnp.cumsum(doc_lengths).astype(jnp.int32)
    start_of = lax.optimization_barrier(jnp.sum(jnp.where(ends[None, :] <= pos[:, None], doc_lengths[None, :], 0), axis=1)).astype(jnp.int32)
    scales_per_token = key_value_scales[pos // SCALE_BLOCK]
    padding_amount = DOC_MOST
    padded_keys = jnp.concatenate([jnp.zeros((padding_amount, KEY_VALUE_HEADS * HEAD_SIZE), keys.dtype), keys], 0).reshape(-1, KEY_VALUE_HEADS, HEAD_SIZE)
    padded_values = jnp.concatenate([jnp.zeros((padding_amount, KEY_VALUE_HEADS * HEAD_SIZE), values.dtype), values], 0).reshape(-1, KEY_VALUE_HEADS, HEAD_SIZE)
    padded_scales = jnp.concatenate([jnp.ones((padding_amount, 2, KEY_VALUE_HEADS), jnp.float32), scales_per_token.astype(jnp.float32)], 0)
    inverse = 1.0 / math.sqrt(HEAD_SIZE)

    def one_block(index):
        query_begin = (index * TOKENS_PER_SHARD).astype(jnp.int32)
        query_rows = lax.dynamic_slice_in_dim(queries, query_begin, TOKENS_PER_SHARD, 0).reshape(TOKENS_PER_SHARD, KEY_VALUE_HEADS, query_group, HEAD_SIZE).astype(jnp.float32)
        kblock = lax.dynamic_slice_in_dim(padded_keys, query_begin, TOKENS_PER_SHARD + padding_amount, 0).astype(jnp.float32)
        vblock = lax.dynamic_slice_in_dim(padded_values, query_begin, TOKENS_PER_SHARD + padding_amount, 0).astype(jnp.float32)
        scales = lax.dynamic_slice_in_dim(padded_scales, query_begin, TOKENS_PER_SHARD + padding_amount, 0)
        qpos = query_begin + jnp.arange(TOKENS_PER_SHARD, dtype=jnp.int32)
        kpos = query_begin - padding_amount + jnp.arange(TOKENS_PER_SHARD + padding_amount, dtype=jnp.int32)
        qstart_of = lax.dynamic_slice_in_dim(start_of, query_begin, TOKENS_PER_SHARD, 0)
        mask = (kpos[None, :] >= qstart_of[:, None]) & (kpos[None, :] <= qpos[:, None])
        score = jnp.einsum('tgjd,sgd->tgjs', query_rows, kblock) * (scales[:, 0, :].T * inverse)[None, :, None, :]
        score = jnp.where(mask[:, None, None, :], score, -jnp.inf)
        top = lax.optimization_barrier(jnp.max(score, axis=-1, keepdims=True))
        prob = jnp.exp(score - top)
        total = lax.optimization_barrier(jnp.sum(prob, axis=-1))
        weighted = (prob * scales[:, 1, :].T[None, :, None, :]).astype(jnp.bfloat16)
        weighted = lax.optimization_barrier(weighted).astype(jnp.float32)
        result = jnp.einsum('tgjs,sgd->tgjd', weighted, vblock) / total[..., None]
        return result.reshape(TOKENS_PER_SHARD, QUERY_HEADS * HEAD_SIZE).astype(jnp.bfloat16)
    blocks = lax.map(one_block, jnp.arange(TRACE_TOKENS // TOKENS_PER_SHARD, dtype=jnp.int32))
    return blocks.reshape(TRACE_TOKENS, QUERY_HEADS * HEAD_SIZE)
```

```python
import functools
import math

import jax
import jax.numpy as jnp
from jax import lax
from jax.experimental import pallas as pl
from jax.experimental.pallas import tpu as pltpu
from jax.sharding import PartitionSpec as P

SCALE_BLOCK = 32
HEAD = 128
ROW = 4
LOW = -1e30
CONTRACT_LAST = (((1,), (1,)), ((), ()))


def attend_kernel(docs, scales, *refs, backs, groups, rows):
    count = len(backs)
    queries, keys, values = refs[0], refs[1 : 1 + count], refs[1 + count : 1 + 2 * count]
    out, mask, kparts, vparts = refs[1 + 2 * count :]
    group = pl.program_id(0)
    first = lax.axis_index("ctx") * rows
    span = count * rows
    heads = queries.shape[1] // HEAD

    @pl.when(group == 0)
    def _():
        qpos = first + lax.broadcasted_iota(jnp.int32, (rows, HEAD), 0)

        def visit(doc, carry):
            end, start = carry
            end = end + docs[doc]
            return end, jnp.where(end <= qpos, end, start)

        _, start = lax.fori_loop(0, docs.shape[0], visit, (0, jnp.zeros((rows, HEAD), jnp.int32)), unroll=8)
        for slot, back in enumerate(backs):
            kpos = first - back * rows + lax.broadcasted_iota(jnp.int32, (rows, rows), 1)
            keep = kpos >= start[:, :1]
            if back == 0:
                keep = keep & (kpos <= qpos[:, :1])
            mask[:, slot * rows : (slot + 1) * rows] = jnp.where(keep, 0.0, LOW)

    lane = lax.broadcasted_iota(jnp.int32, (SCALE_BLOCK, HEAD), 1)
    wide = lax.broadcasted_iota(jnp.int32, (1, rows), 1)
    level = []
    for slot, back in enumerate(backs):
        line = jnp.zeros((1, rows), jnp.float32)
        for piece in range(rows // SCALE_BLOCK):
            block = jnp.maximum(first // SCALE_BLOCK - back * (rows // SCALE_BLOCK) + piece, 0)
            kscale = scales[block * 2 * groups + group] * (math.log2(math.e) / math.sqrt(HEAD))
            vscale = scales[block * 2 * groups + groups + group]
            source = pl.ds(piece * SCALE_BLOCK, SCALE_BLOCK)
            target = pl.ds(slot * rows + piece * SCALE_BLOCK, SCALE_BLOCK)
            scaled = keys[slot][source, :].astype(jnp.float32) * kscale
            high = scaled.astype(jnp.bfloat16)
            kparts[target, :HEAD] = high
            kparts[target, HEAD:] = (scaled - high.astype(jnp.float32)).astype(jnp.bfloat16)
            inverse = 1.0 / jnp.full((SCALE_BLOCK, HEAD), vscale, jnp.float32)
            high = inverse.astype(jnp.bfloat16).astype(jnp.float32)
            ones = jnp.where(lane == 0, high, jnp.where(lane == 1, inverse - high, 0.0))
            vparts[target, :HEAD] = values[slot][source, :]
            vparts[target, HEAD:] = ones.astype(jnp.bfloat16)
            line = jnp.where(wide // SCALE_BLOCK == piece, vscale, line)
        level.append(jnp.log2(line))
    bias = mask[...] + jnp.concatenate(level, axis=1)

    query = jnp.concatenate([queries[:, h * HEAD : (h + 1) * HEAD] for h in range(heads)], axis=0)
    query = jnp.concatenate([query, query], axis=1)
    score = lax.dot_general(query, kparts[...], CONTRACT_LAST, preferred_element_type=jnp.float32)
    score = score.reshape(heads, rows, span) + bias[None]
    top = jnp.max(score, axis=-1, keepdims=True)
    weighted = jnp.exp2(score - top).astype(jnp.bfloat16).reshape(heads * rows, span)
    both = jnp.dot(weighted, vparts[...], preferred_element_type=jnp.float32)
    total = both[:, HEAD : HEAD + 1] + both[:, HEAD + 1 : HEAD + 2]
    result = (both[:, :HEAD] / total).astype(jnp.bfloat16)
    for h in range(heads):
        out[:, h * HEAD : (h + 1) * HEAD] = result[h * rows : (h + 1) * rows]


def attend(docs, scales, queries, blocks, backs):
    rows, width = queries.shape
    groups = blocks[0].shape[1] // (2 * HEAD)
    count = len(backs)
    span = count * rows
    per = width // groups
    smem = pl.BlockSpec(memory_space=pltpu.SMEM)
    return pl.pallas_call(
        functools.partial(attend_kernel, backs=backs, groups=groups, rows=rows),
        grid=(groups,),
        in_specs=[smem, smem, pl.BlockSpec((rows, per), lambda g: (0, g))]
        + [pl.BlockSpec((rows, HEAD), lambda g: (0, g))] * count
        + [pl.BlockSpec((rows, HEAD), lambda g: (0, groups + g))] * count,
        out_specs=pl.BlockSpec((rows, per), lambda g: (0, g)),
        out_shape=jax.ShapeDtypeStruct((rows, width), jnp.bfloat16),
        scratch_shapes=[
            pltpu.VMEM((rows, span), jnp.float32),
            pltpu.VMEM((span, 2 * HEAD), jnp.bfloat16),
            pltpu.VMEM((span, 2 * HEAD), jnp.bfloat16),
        ],
        compiler_params=pltpu.CompilerParams(vmem_limit_bytes=48 * 2**20),
    )(docs, scales, queries, *blocks, *blocks)


def ahead(block, distance):
    size = lax.axis_size("ctx")
    return lax.ppermute(block, "ctx", [(i, i + distance) for i in range(size - distance)])


def in_row(block, step):
    size = lax.axis_size("ctx")
    return lax.ppermute(block, "ctx", [(i, i // ROW * ROW + (i + step) % ROW) for i in range(size)])


def per_device(queries, keys, values, key_value_scales, doc_lengths):
    own = jnp.concatenate([keys, values], axis=1)
    column = lax.axis_index("ctx") % ROW
    fourth = ahead(own, 4)
    second = ahead(own, 2)
    third = in_row(jnp.where(column == 0, own, fourth), ROW - 1)
    nearest = in_row(jnp.where(column < ROW - 1, own, fourth), 1)
    scales = key_value_scales.reshape(-1)
    blocks = (own, fourth, second, third, nearest)
    return attend(doc_lengths, scales, queries, blocks, (0, 4, 2, 3, 1))


def solution(mesh):
    return jax.shard_map(
        per_device,
        mesh=mesh,
        in_specs=(
            P(("seq", "ctx"), None),
            P(("seq", "ctx"), None),
            P(("seq", "ctx"), None),
            P("seq", None, None),
            P("seq"),
        ),
        out_specs=P(("seq", "ctx"), None),
        check_vma=False,
    )
```

```python
import functools
import math

import jax
import jax.numpy as jnp
from jax import lax
from jax.experimental import pallas as pl
from jax.experimental.pallas import tpu as pltpu
from jax.sharding import PartitionSpec as P

SCALE_BLOCK = 32
HEAD = 128
LOW = -1e30
LAST = (((1,), (1,)), ((), ()))
EXTRA = 16
CHUNK = 8
ROW = 4


def table_kernel(docs, scales, table, *, groups, rows, backs):
    first = lax.axis_index("ctx") * rows
    pieces = rows // SCALE_BLOCK
    qpos = first + lax.broadcasted_iota(jnp.int32, (8, rows), 1)

    def visit(doc, carry):
        end, start = carry
        end = end + docs[doc]
        return end, jnp.where(end <= qpos, end, start)

    _, start = lax.fori_loop(0, docs.shape[0], visit, (0, jnp.zeros((8, rows), jnp.int32)), unroll=8)
    lane = lax.broadcasted_iota(jnp.int32, (1, rows), 1) // SCALE_BLOCK
    for slot, back in enumerate(backs):
        kpos = first - back * rows + lax.broadcasted_iota(jnp.int32, (rows, rows), 0)
        keep = kpos >= start[:1]
        if back == 0:
            keep = keep & (kpos <= qpos[:1])
        table[slot, :rows, :] = jnp.where(keep, 0.0, LOW)
        for group in range(groups):
            line = jnp.ones((1, rows), jnp.float32)
            for piece in range(pieces):
                block = jnp.maximum(first // SCALE_BLOCK - back * pieces + piece, 0)
                kscale = scales[block * 2 * groups + group] * (math.log2(math.e) / math.sqrt(HEAD))
                vscale = scales[block * 2 * groups + groups + group]
                at = rows + group * (2 * pieces + 1) + 2 * piece
                table[slot, at : at + 1, :] = jnp.full((1, rows), kscale, jnp.float32)
                table[slot, at + 1 : at + 2, :] = jnp.log2(jnp.full((1, rows), vscale, jnp.float32))
                line = jnp.where(lane == piece, vscale, line)
            at = rows + group * (2 * pieces + 1) + 2 * pieces
            table[slot, at : at + 1, :] = 1.0 / line


def make_table(docs, scales, rows, groups, backs):
    depth = rows + groups * (2 * (rows // SCALE_BLOCK) + 1)
    depth = (depth + 7) // 8 * 8
    smem = pl.BlockSpec(memory_space=pltpu.SMEM)
    return pl.pallas_call(
        functools.partial(table_kernel, groups=groups, rows=rows, backs=backs),
        in_specs=[smem, smem],
        out_specs=pl.BlockSpec(memory_space=pltpu.VMEM),
        out_shape=jax.ShapeDtypeStruct((len(backs), depth, rows), jnp.float32),
    )(docs, scales)


def kernel(*refs, slots, groups, rows, state, final, chunk):
    count = len(slots)
    refs = list(refs)
    sources = refs[: 2 + count + 2 * state]
    refs = refs[len(sources) :]
    if final:
        out = refs[0]
        refs = refs[1:]
    else:
        acc_out, stat_out = refs[:2]
        refs = refs[2:]
    buffers = sources
    bias, kparts, vparts, scores, probs = refs[:5]
    if final:
        stage, out_sems = refs[5:]
    width = sources[1].shape[1]
    heads = width // HEAD
    per = heads // groups
    pieces = rows // SCALE_BLOCK

    table, queries, blocks = buffers[0], buffers[1], buffers[2 : 2 + count]
    if state:
        acc_in, stat_in = buffers[2 + count], buffers[3 + count]

    deep = lax.broadcasted_iota(jnp.int32, (EXTRA, rows), 0)

    def prepare(group):
        at = group % 3
        for slot in range(count):
            base = rows + group * (2 * pieces + 1)
            for piece in range(pieces):
                source = pl.ds(piece * SCALE_BLOCK, SCALE_BLOCK)
                target = pl.ds(slot * rows + piece * SCALE_BLOCK, SCALE_BLOCK)
                kscale = table[slots[slot], base + 2 * piece : base + 2 * piece + 1, :]
                scaled = blocks[slot][source, group * HEAD : (group + 1) * HEAD].astype(jnp.float32) * kscale
                high = scaled.astype(jnp.bfloat16)
                kparts[at, target, :HEAD] = high
                kparts[at, target, HEAD:] = (scaled - high.astype(jnp.float32)).astype(jnp.bfloat16)
                bias[at, target, :] = table[slots[slot], source, :] + table[slots[slot], base + 2 * piece + 1 : base + 2 * piece + 2, :]
            inverse = table[slots[slot], base + 2 * pieces : base + 2 * pieces + 1, :]
            high = inverse.astype(jnp.bfloat16).astype(jnp.float32)
            ones = jnp.where(deep == 0, high, jnp.where(deep == 1, inverse - high, 0.0))
            columns = pl.ds(slot * rows, rows)
            vparts[at, :HEAD, columns] = blocks[slot][:, (groups + group) * HEAD : (groups + group + 1) * HEAD].T
            vparts[at, HEAD:, columns] = ones.astype(jnp.bfloat16)

    steps = heads // chunk
    tops = {}

    def some(step):
        return range(step * chunk, (step + 1) * chunk)

    def across(ref, offset, step):
        return jnp.concatenate([ref[offset + h : offset + h + 1, :] for h in some(step)], axis=1)

    def score_part(step):
        group = step * chunk // per
        if step * chunk % per == 0:
            prepare(group)
        query = jnp.concatenate([queries[:, h * HEAD : (h + 1) * HEAD] for h in some(step)], axis=0)
        query = jnp.concatenate([query, query], axis=1)
        score = lax.dot_general(kparts[group % 3], query, LAST, preferred_element_type=jnp.float32)
        score = score + jnp.concatenate([bias[group % 3]] * chunk, axis=1)
        scores[step % 2] = score
        top = jnp.max(score, axis=0, keepdims=True)
        if state:
            top = jnp.maximum(top, across(stat_in, 0, step))
        tops[step] = top

    def prob_part(step):
        probs[step % 2] = jnp.exp2(scores[step % 2] - tops[step]).astype(jnp.bfloat16)

    def send(group):
        columns = pl.ds(group * per * HEAD, per * HEAD)
        return pltpu.make_async_copy(stage.at[:, columns], out.at[:, columns], out_sems.at[group])

    def value_part(step):
        group = step * chunk // per
        both = jnp.dot(vparts[group % 3], probs[step % 2], preferred_element_type=jnp.float32)
        total = both[HEAD : HEAD + 1] + both[HEAD + 1 : HEAD + 2]
        result = both[:HEAD]
        if state:
            keep = jnp.exp2(across(stat_in, 0, step) - tops[step])
            total = total + keep * across(stat_in, heads, step)
            old = jnp.concatenate([acc_in[h * HEAD : (h + 1) * HEAD, :] for h in some(step)], axis=1)
            result = result + keep * old
        if final:
            result = result * (1.0 / total)
        for at, h in enumerate(some(step)):
            lanes = slice(at * rows, (at + 1) * rows)
            if final:
                stage[:, h * HEAD : (h + 1) * HEAD] = result[:, lanes].T.astype(jnp.bfloat16)
            else:
                acc_out[h * HEAD : (h + 1) * HEAD, :] = result[:, lanes]
                stat_out[h : h + 1, :] = tops[step][:, lanes]
                stat_out[heads + h : heads + h + 1, :] = total[:, lanes]
        if final and (step + 1) * chunk % per == 0:
            send(group).start()

    for step in range(steps + 2):
        if step < steps:
            score_part(step)
        if 1 <= step <= steps:
            prob_part(step - 1)
        if 2 <= step:
            value_part(step - 2)
    if final:
        for group in range(groups):
            send(group).wait()


def attend(table, queries, blocks, slots, state=None, final=True, chunk=CHUNK):
    rows, width = queries.shape
    groups = blocks[0].shape[1] // (2 * HEAD)
    count = len(slots)
    span = count * rows
    heads = width // HEAD
    anywhere = pl.BlockSpec(memory_space=pl.ANY)
    state_shapes = [
        jax.ShapeDtypeStruct((width, rows), jnp.float32),
        jax.ShapeDtypeStruct((2 * heads, rows), jnp.float32),
    ]
    held = state is not None
    scratch = []
    scratch += [
        pltpu.VMEM((3, span, rows), jnp.float32),
        pltpu.VMEM((3, span, 2 * HEAD), jnp.bfloat16),
        pltpu.VMEM((3, HEAD + EXTRA, span), jnp.bfloat16),
        pltpu.VMEM((2, span, chunk * rows), jnp.float32),
        pltpu.VMEM((2, span, chunk * rows), jnp.bfloat16),
    ]
    if final:
        scratch += [pltpu.VMEM((rows, width), jnp.bfloat16), pltpu.SemaphoreType.DMA((groups,))]
    return pl.pallas_call(
        functools.partial(kernel, slots=slots, groups=groups, rows=rows, state=held, final=final, chunk=chunk),
        in_specs=[pl.BlockSpec(memory_space=pltpu.VMEM)] * (2 + count + 2 * held),
        out_specs=anywhere if final else [pl.BlockSpec(memory_space=pltpu.VMEM)] * 2,
        out_shape=jax.ShapeDtypeStruct((rows, width), jnp.bfloat16) if final else state_shapes,
        scratch_shapes=scratch,
        compiler_params=pltpu.CompilerParams(vmem_limit_bytes=40 * 2**20),
        cost_estimate=pl.CostEstimate(
            flops=4 * rows * width * span, bytes_accessed=4 * rows * width, transcendentals=heads * rows * span
        ),
    )(table, queries, *blocks, *(state if held else ()))


def ahead(block, distance):
    size = lax.axis_size("ctx")
    return lax.ppermute(block, "ctx", [(i, i + distance) for i in range(size - distance)])


def in_row(block, step):
    size = lax.axis_size("ctx")
    return lax.ppermute(block, "ctx", [(i, i // ROW * ROW + (i + step) % ROW) for i in range(size)])


def per_device(queries, keys, values, key_value_scales, doc_lengths):
    rows = queries.shape[0]
    groups = key_value_scales.shape[2]
    own = jnp.concatenate([keys, values], axis=1)
    column = lax.axis_index("ctx") % ROW
    fourth = ahead(own, 4)
    second = ahead(own, 2)
    third = in_row(jnp.where(column == 0, own, fourth), ROW - 1)
    nearest = in_row(jnp.where(column < ROW - 1, own, fourth), 1)
    table = make_table(doc_lengths, key_value_scales.reshape(-1), rows, groups, (0, 4, 2, 3, 1))
    state = attend(table, queries, (own, fourth, second), (0, 1, 2), final=False)
    state = attend(table, queries, (third,), (3,), state=state, final=False)
    return attend(table, queries, (nearest,), (4,), state=state)


def solution(mesh):
    return jax.shard_map(
        per_device,
        mesh=mesh,
        in_specs=(
            P(("seq", "ctx"), None),
            P(("seq", "ctx"), None),
            P(("seq", "ctx"), None),
            P("seq", None, None),
            P("seq"),
        ),
        out_specs=P(("seq", "ctx"), None),
        check_vma=False,
    )
```

```python
import functools
import math

import jax
import jax.numpy as jnp
from jax import lax
from jax.experimental import pallas as pl
from jax.experimental.pallas import tpu as pltpu
from jax.sharding import PartitionSpec as P

SCALE_BLOCK = 32
HEAD = 128
LOW = -1e30
LAST = (((1,), (1,)), ((), ()))
EXTRA = 16
CHUNK = 8
ROW = 4


def join_kernel(keys, values, own, other, sems):
    half = keys.shape[1]
    copies = [
        pltpu.make_async_copy(source, target.at[:, pl.ds(at * half, half)], sems.at[2 * number + at])
        for number, target in enumerate((own, other))
        for at, source in enumerate((keys, values))
    ]
    for copy in copies:
        copy.start()
    for copy in copies:
        copy.wait()


def join(keys, values):
    rows, half = keys.shape
    vmem = pl.BlockSpec(memory_space=pltpu.VMEM)
    return pl.pallas_call(
        join_kernel,
        in_specs=[pl.BlockSpec(memory_space=pl.ANY)] * 2,
        out_specs=[vmem, vmem],
        out_shape=[jax.ShapeDtypeStruct((rows, 2 * half), keys.dtype)] * 2,
        scratch_shapes=[pltpu.SemaphoreType.DMA((4,))],
    )(keys, values)


def table_kernel(docs, scales, passed_in, table, passed, *, groups, rows, backs):
    del passed_in, passed
    first = lax.axis_index("ctx") * rows
    pieces = rows // SCALE_BLOCK
    qpos = first + lax.broadcasted_iota(jnp.int32, (8, rows), 1)

    def visit(doc, carry):
        end, start = carry
        end = end + docs[doc]
        return end, jnp.where(end <= qpos, end, start)

    _, start = lax.fori_loop(0, docs.shape[0], visit, (0, jnp.zeros((8, rows), jnp.int32)), unroll=8)
    both = jnp.concatenate([scales[0], scales[1]], axis=0)
    place = lax.broadcasted_iota(jnp.int32, both.shape, 1)
    lane = lax.broadcasted_iota(jnp.int32, (2 * groups, rows), 1) // SCALE_BLOCK
    upper = lax.broadcasted_iota(jnp.int32, (2 * groups, rows), 0) < groups
    for slot, back in enumerate(backs):
        kpos = first - back * rows + lax.broadcasted_iota(jnp.int32, (rows, rows), 0)
        keep = kpos >= start[:1]
        if back == 0:
            keep = keep & (kpos <= qpos[:1])
        table[slot, :rows, :] = jnp.where(keep, 0.0, LOW)
        line = jnp.ones((2 * groups, rows), jnp.float32)
        for piece in range(pieces):
            block = jnp.maximum(first // SCALE_BLOCK - back * pieces + piece, 0)
            column = jnp.sum(jnp.where(place == block, both, 0.0), axis=1, keepdims=True)
            wide = jnp.broadcast_to(column, (2 * groups, rows))
            at = rows + 2 * groups * piece
            table[slot, at : at + 2 * groups, :] = jnp.where(
                upper, wide * (math.log2(math.e) / math.sqrt(HEAD)), jnp.log2(wide)
            )
            line = jnp.where(lane == piece, wide, line)
        at = rows + 2 * groups * pieces
        table[slot, at : at + 2 * groups, :] = 1.0 / line


def make_table(docs, scales, passed, rows, groups, backs):
    depth = rows + 2 * groups * (rows // SCALE_BLOCK + 1)
    vmem = pl.BlockSpec(memory_space=pltpu.VMEM)
    anywhere = pl.BlockSpec(memory_space=pl.ANY)
    return pl.pallas_call(
        functools.partial(table_kernel, groups=groups, rows=rows, backs=backs),
        in_specs=[pl.BlockSpec(memory_space=pltpu.SMEM), vmem, anywhere],
        out_specs=[vmem, anywhere],
        out_shape=[
            jax.ShapeDtypeStruct((len(backs), depth, rows), jnp.float32),
            jax.ShapeDtypeStruct(passed.shape, passed.dtype),
        ],
        input_output_aliases={2: 1},
    )(docs, scales.transpose(1, 2, 0), passed)


def kernel(*refs, slots, groups, rows, state, final, chunk):
    count = len(slots)
    refs = list(refs)
    sources = refs[: 2 + count + 2 * state]
    refs = refs[len(sources) :]
    if final:
        out = refs[0]
        refs = refs[1:]
    else:
        acc_out, stat_out = refs[:2]
        refs = refs[2:]
    buffers = sources
    bias, kparts, vparts, scores, probs = refs[:5]
    if final:
        stage, out_sems = refs[5:]
    width = sources[1].shape[1]
    heads = width // HEAD
    per = heads // groups
    pieces = rows // SCALE_BLOCK

    table, queries, blocks = buffers[0], buffers[1], buffers[2 : 2 + count]
    if state:
        acc_in, stat_in = buffers[2 + count], buffers[3 + count]

    deep = lax.broadcasted_iota(jnp.int32, (EXTRA, rows), 0)

    def prepare(group):
        at = group % 3
        for slot in range(count):
            for piece in range(pieces):
                source = pl.ds(piece * SCALE_BLOCK, SCALE_BLOCK)
                target = pl.ds(slot * rows + piece * SCALE_BLOCK, SCALE_BLOCK)
                base = rows + 2 * groups * piece + group
                kscale = table[slots[slot], base : base + 1, :]
                scaled = blocks[slot][source, group * HEAD : (group + 1) * HEAD].astype(jnp.float32) * kscale
                high = scaled.astype(jnp.bfloat16)
                kparts[at, target, :HEAD] = high
                kparts[at, target, HEAD:] = (scaled - high.astype(jnp.float32)).astype(jnp.bfloat16)
                bias[at, target, :] = table[slots[slot], source, :] + table[slots[slot], base + groups : base + groups + 1, :]
            base = rows + 2 * groups * pieces + groups + group
            inverse = table[slots[slot], base : base + 1, :]
            high = inverse.astype(jnp.bfloat16).astype(jnp.float32)
            ones = jnp.where(deep == 0, high, jnp.where(deep == 1, inverse - high, 0.0))
            columns = pl.ds(slot * rows, rows)
            vparts[at, :HEAD, columns] = blocks[slot][:, (groups + group) * HEAD : (groups + group + 1) * HEAD].T
            vparts[at, HEAD:, columns] = ones.astype(jnp.bfloat16)

    steps = heads // chunk
    tops = {}

    def some(step):
        return range(step * chunk, (step + 1) * chunk)

    def across(ref, offset, step):
        return jnp.concatenate([ref[offset + h : offset + h + 1, :] for h in some(step)], axis=1)

    def score_part(step):
        group = step * chunk // per
        if step * chunk % per == 0:
            prepare(group)
        query = jnp.concatenate([queries[:, h * HEAD : (h + 1) * HEAD] for h in some(step)], axis=0)
        query = jnp.concatenate([query, query], axis=1)
        score = lax.dot_general(kparts[group % 3], query, LAST, preferred_element_type=jnp.float32)
        score = score + jnp.concatenate([bias[group % 3]] * chunk, axis=1)
        scores[step % 2] = score
        top = jnp.max(score, axis=0, keepdims=True)
        if state:
            top = jnp.maximum(top, across(stat_in, 0, step))
        tops[step] = top

    def prob_part(step):
        probs[step % 2] = jnp.exp2(scores[step % 2] - tops[step]).astype(jnp.bfloat16)

    def send(group):
        columns = pl.ds(group * per * HEAD, per * HEAD)
        return pltpu.make_async_copy(stage.at[:, columns], out.at[:, columns], out_sems.at[group])

    def value_part(step):
        group = step * chunk // per
        both = jnp.dot(vparts[group % 3], probs[step % 2], preferred_element_type=jnp.float32)
        total = both[HEAD : HEAD + 1] + both[HEAD + 1 : HEAD + 2]
        result = both[:HEAD]
        if state:
            keep = jnp.exp2(across(stat_in, 0, step) - tops[step])
            total = total + keep * across(stat_in, heads, step)
            old = jnp.concatenate([acc_in[h * HEAD : (h + 1) * HEAD, :] for h in some(step)], axis=1)
            result = result + keep * old
        if final:
            result = result * (1.0 / total)
        for at, h in enumerate(some(step)):
            lanes = slice(at * rows, (at + 1) * rows)
            if final:
                stage[:, h * HEAD : (h + 1) * HEAD] = result[:, lanes].T.astype(jnp.bfloat16)
            else:
                acc_out[h * HEAD : (h + 1) * HEAD, :] = result[:, lanes]
                stat_out[h : h + 1, :] = tops[step][:, lanes]
                stat_out[heads + h : heads + h + 1, :] = total[:, lanes]
        if final and (step + 1) * chunk % per == 0:
            send(group).start()

    for step in range(steps + 2):
        if step < steps:
            score_part(step)
        if 1 <= step <= steps:
            prob_part(step - 1)
        if 2 <= step:
            value_part(step - 2)
    if final:
        for group in range(groups):
            send(group).wait()


def attend(table, queries, blocks, slots, state=None, final=True, chunk=CHUNK):
    rows, width = queries.shape
    groups = blocks[0].shape[1] // (2 * HEAD)
    count = len(slots)
    span = count * rows
    heads = width // HEAD
    anywhere = pl.BlockSpec(memory_space=pl.ANY)
    state_shapes = [
        jax.ShapeDtypeStruct((width, rows), jnp.float32),
        jax.ShapeDtypeStruct((2 * heads, rows), jnp.float32),
    ]
    held = state is not None
    scratch = []
    scratch += [
        pltpu.VMEM((3, span, rows), jnp.float32),
        pltpu.VMEM((3, span, 2 * HEAD), jnp.bfloat16),
        pltpu.VMEM((3, HEAD + EXTRA, span), jnp.bfloat16),
        pltpu.VMEM((2, span, chunk * rows), jnp.float32),
        pltpu.VMEM((2, span, chunk * rows), jnp.bfloat16),
    ]
    if final:
        scratch += [pltpu.VMEM((rows, width), jnp.bfloat16), pltpu.SemaphoreType.DMA((groups,))]
    return pl.pallas_call(
        functools.partial(kernel, slots=slots, groups=groups, rows=rows, state=held, final=final, chunk=chunk),
        in_specs=[pl.BlockSpec(memory_space=pltpu.VMEM)] * (2 + count + 2 * held),
        out_specs=anywhere if final else [pl.BlockSpec(memory_space=pltpu.VMEM)] * 2,
        out_shape=jax.ShapeDtypeStruct((rows, width), jnp.bfloat16) if final else state_shapes,
        scratch_shapes=scratch,
        compiler_params=pltpu.CompilerParams(vmem_limit_bytes=40 * 2**20),
        cost_estimate=pl.CostEstimate(
            flops=4 * rows * width * span, bytes_accessed=4 * rows * width, transcendentals=heads * rows * span
        ),
    )(table, queries, *blocks, *(state if held else ()))


def ahead(block, distance):
    size = lax.axis_size("ctx")
    return lax.ppermute(block, "ctx", [(i, i + distance) for i in range(size - distance)])


def in_row(block, step):
    size = lax.axis_size("ctx")
    return lax.ppermute(block, "ctx", [(i, i // ROW * ROW + (i + step) % ROW) for i in range(size)])


def per_device(queries, keys, values, key_value_scales, doc_lengths):
    rows = queries.shape[0]
    groups = key_value_scales.shape[2]
    own, other = join(keys, values)
    column = lax.axis_index("ctx") % ROW
    fourth = ahead(own, 4)
    table, other = make_table(doc_lengths, key_value_scales, other, rows, groups, (0, 4, 2, 3, 1))
    second = ahead(other, 2)
    third = in_row(jnp.where(column == 0, own, fourth), ROW - 1)
    nearest = in_row(jnp.where(column < ROW - 1, own, fourth), 1)
    state = attend(table, queries, (own, fourth, second), (0, 1, 2), final=False)
    state = attend(table, queries, (third,), (3,), state=state, final=False)
    return attend(table, queries, (nearest,), (4,), state=state)


def solution(mesh):
    return jax.shard_map(
        per_device,
        mesh=mesh,
        in_specs=(
            P(("seq", "ctx"), None),
            P(("seq", "ctx"), None),
            P(("seq", "ctx"), None),
            P("seq", None, None),
            P("seq"),
        ),
        out_specs=P(("seq", "ctx"), None),
        check_vma=False,
    )
```

```python
import functools
import math

import jax
import jax.numpy as jnp
from jax import lax
from jax.experimental import pallas as pl
from jax.experimental.pallas import tpu as pltpu
from jax.sharding import PartitionSpec as P

SCALE_BLOCK = 32
HEAD = 128
LOW = -1e30
LAST = (((1,), (1,)), ((), ()))
EXTRA = 16
CHUNK = 8
ROW = 4


def join_kernel(keys, values, own, other, sems):
    half = keys.shape[1]
    copies = [
        pltpu.make_async_copy(source, target.at[:, pl.ds(at * half, half)], sems.at[2 * number + at])
        for number, target in enumerate((own, other))
        for at, source in enumerate((keys, values))
    ]
    for copy in copies:
        copy.start()
    for copy in copies:
        copy.wait()


def join(keys, values):
    rows, half = keys.shape
    vmem = pl.BlockSpec(memory_space=pltpu.VMEM)
    return pl.pallas_call(
        join_kernel,
        in_specs=[pl.BlockSpec(memory_space=pl.ANY)] * 2,
        out_specs=[vmem, vmem],
        out_shape=[jax.ShapeDtypeStruct((rows, 2 * half), keys.dtype)] * 2,
        scratch_shapes=[pltpu.SemaphoreType.DMA((4,))],
        compiler_params=pltpu.CompilerParams(vmem_limit_bytes=4 * 2**20),
    )(keys, values)


def table_kernel(docs, scales, passed_in, table, passed, *, groups, rows, backs):
    del passed_in, passed
    first = lax.axis_index("ctx") * rows
    pieces = rows // SCALE_BLOCK
    qpos = first + lax.broadcasted_iota(jnp.int32, (8, rows), 1)

    def visit(doc, carry):
        end, start = carry
        end = end + docs[doc]
        return end, jnp.where(end <= qpos, end, start)

    _, start = lax.fori_loop(0, docs.shape[0], visit, (0, jnp.zeros((8, rows), jnp.int32)), unroll=8)
    both = jnp.concatenate([scales[0], scales[1]], axis=0)
    place = lax.broadcasted_iota(jnp.int32, both.shape, 1)
    lane = lax.broadcasted_iota(jnp.int32, (2 * groups, rows), 1) // SCALE_BLOCK
    upper = lax.broadcasted_iota(jnp.int32, (2 * groups, rows), 0) < groups
    for slot, back in enumerate(backs):
        kpos = first - back * rows + lax.broadcasted_iota(jnp.int32, (rows, rows), 0)
        keep = kpos >= start[:1]
        if back == 0:
            keep = keep & (kpos <= qpos[:1])
        table[slot, :rows, :] = jnp.where(keep, 0.0, LOW)
        line = jnp.ones((2 * groups, rows), jnp.float32)
        for piece in range(pieces):
            block = jnp.maximum(first // SCALE_BLOCK - back * pieces + piece, 0)
            column = jnp.sum(jnp.where(place == block, both, 0.0), axis=1, keepdims=True)
            wide = jnp.broadcast_to(column, (2 * groups, rows))
            at = rows + 2 * groups * piece
            table[slot, at : at + 2 * groups, :] = jnp.where(
                upper, wide * (math.log2(math.e) / math.sqrt(HEAD)), jnp.log2(wide)
            )
            line = jnp.where(lane == piece, wide, line)
        at = rows + 2 * groups * pieces
        table[slot, at : at + 2 * groups, :] = 1.0 / line


def make_table(docs, scales, passed, rows, groups, backs):
    depth = rows + 2 * groups * (rows // SCALE_BLOCK + 1)
    vmem = pl.BlockSpec(memory_space=pltpu.VMEM)
    anywhere = pl.BlockSpec(memory_space=pl.ANY)
    return pl.pallas_call(
        functools.partial(table_kernel, groups=groups, rows=rows, backs=backs),
        in_specs=[pl.BlockSpec(memory_space=pltpu.SMEM), vmem, anywhere],
        out_specs=[vmem, anywhere],
        out_shape=[
            jax.ShapeDtypeStruct((len(backs), depth, rows), jnp.float32),
            jax.ShapeDtypeStruct(passed.shape, passed.dtype),
        ],
        input_output_aliases={2: 1},
        compiler_params=pltpu.CompilerParams(vmem_limit_bytes=4 * 2**20),
    )(docs, scales.transpose(1, 2, 0), passed)


def kernel(*refs, slots, groups, rows, state, final, chunk):
    count = len(slots)
    refs = list(refs)
    sources = refs[: 2 + count + 2 * state]
    refs = refs[len(sources) :]
    if final:
        out = refs[0]
        refs = refs[1:]
    else:
        acc_out, stat_out = refs[:2]
        refs = refs[2:]
    buffers = sources
    bias, kparts, vparts, scores, probs = refs[:5]
    if final:
        stage, out_sems = refs[5:]
    width = sources[1].shape[1]
    heads = width // HEAD
    per = heads // groups
    pieces = rows // SCALE_BLOCK

    table, queries, blocks = buffers[0], buffers[1], buffers[2 : 2 + count]
    if state:
        acc_in, stat_in = buffers[2 + count], buffers[3 + count]

    deep = lax.broadcasted_iota(jnp.int32, (EXTRA, rows), 0)

    def prepare(group):
        at = group % 3
        for slot in range(count):
            for piece in range(pieces):
                source = pl.ds(piece * SCALE_BLOCK, SCALE_BLOCK)
                target = pl.ds(slot * rows + piece * SCALE_BLOCK, SCALE_BLOCK)
                base = rows + 2 * groups * piece + group
                kscale = table[slots[slot], base : base + 1, :]
                scaled = blocks[slot][source, group * HEAD : (group + 1) * HEAD].astype(jnp.float32) * kscale
                high = scaled.astype(jnp.bfloat16)
                kparts[at, target, :HEAD] = high
                kparts[at, target, HEAD:] = (scaled - high.astype(jnp.float32)).astype(jnp.bfloat16)
                bias[at, target, :] = table[slots[slot], source, :] + table[slots[slot], base + groups : base + groups + 1, :]
            base = rows + 2 * groups * pieces + groups + group
            inverse = table[slots[slot], base : base + 1, :]
            high = inverse.astype(jnp.bfloat16).astype(jnp.float32)
            ones = jnp.where(deep == 0, high, jnp.where(deep == 1, inverse - high, 0.0))
            columns = pl.ds(slot * rows, rows)
            vparts[at, :HEAD, columns] = blocks[slot][:, (groups + group) * HEAD : (groups + group + 1) * HEAD].T
            vparts[at, HEAD:, columns] = ones.astype(jnp.bfloat16)

    steps = heads // chunk
    tops = {}

    def some(step):
        return range(step * chunk, (step + 1) * chunk)

    def across(ref, offset, step):
        return jnp.concatenate([ref[offset + h : offset + h + 1, :] for h in some(step)], axis=1)

    def score_part(step):
        group = step * chunk // per
        if step * chunk % per == 0:
            prepare(group)
        query = jnp.concatenate([queries[:, h * HEAD : (h + 1) * HEAD] for h in some(step)], axis=0)
        query = jnp.concatenate([query, query], axis=1)
        score = lax.dot_general(kparts[group % 3], query, LAST, preferred_element_type=jnp.float32)
        score = score + jnp.concatenate([bias[group % 3]] * chunk, axis=1)
        scores[step % 2] = score
        top = jnp.max(score, axis=0, keepdims=True)
        if state:
            top = jnp.maximum(top, across(stat_in, 0, step))
        tops[step] = top

    def prob_part(step):
        probs[step % 2] = jnp.exp2(scores[step % 2] - tops[step]).astype(jnp.bfloat16)

    def send(group):
        columns = pl.ds(group * per * HEAD, per * HEAD)
        return pltpu.make_async_copy(stage.at[:, columns], out.at[:, columns], out_sems.at[group])

    def value_part(step):
        group = step * chunk // per
        both = jnp.dot(vparts[group % 3], probs[step % 2], preferred_element_type=jnp.float32)
        total = both[HEAD : HEAD + 1] + both[HEAD + 1 : HEAD + 2]
        result = both[:HEAD]
        if state:
            keep = jnp.exp2(across(stat_in, 0, step) - tops[step])
            total = total + keep * across(stat_in, heads, step)
            old = jnp.concatenate([acc_in[h * HEAD : (h + 1) * HEAD, :] for h in some(step)], axis=1)
            result = result + keep * old
        if final:
            result = result * (1.0 / total)
        for at, h in enumerate(some(step)):
            lanes = slice(at * rows, (at + 1) * rows)
            if final:
                stage[:, h * HEAD : (h + 1) * HEAD] = result[:, lanes].T.astype(jnp.bfloat16)
            else:
                acc_out[h * HEAD : (h + 1) * HEAD, :] = result[:, lanes]
                stat_out[h : h + 1, :] = tops[step][:, lanes]
                stat_out[heads + h : heads + h + 1, :] = total[:, lanes]
        if final and (step + 1) * chunk % per == 0:
            send(group).start()

    for step in range(steps + 2):
        if step < steps:
            score_part(step)
        if 1 <= step <= steps:
            prob_part(step - 1)
        if 2 <= step:
            value_part(step - 2)
    if final:
        for group in range(groups):
            send(group).wait()


def attend(table, queries, blocks, slots, state=None, final=True, chunk=CHUNK):
    rows, width = queries.shape
    groups = blocks[0].shape[1] // (2 * HEAD)
    count = len(slots)
    span = count * rows
    heads = width // HEAD
    anywhere = pl.BlockSpec(memory_space=pl.ANY)
    state_shapes = [
        jax.ShapeDtypeStruct((width, rows), jnp.float32),
        jax.ShapeDtypeStruct((2 * heads, rows), jnp.float32),
    ]
    held = state is not None
    scratch = []
    scratch += [
        pltpu.VMEM((3, span, rows), jnp.float32),
        pltpu.VMEM((3, span, 2 * HEAD), jnp.bfloat16),
        pltpu.VMEM((3, HEAD + EXTRA, span), jnp.bfloat16),
        pltpu.VMEM((2, span, chunk * rows), jnp.float32),
        pltpu.VMEM((2, span, chunk * rows), jnp.bfloat16),
    ]
    if final:
        scratch += [pltpu.VMEM((rows, width), jnp.bfloat16), pltpu.SemaphoreType.DMA((groups,))]
    return pl.pallas_call(
        functools.partial(kernel, slots=slots, groups=groups, rows=rows, state=held, final=final, chunk=chunk),
        in_specs=[pl.BlockSpec(memory_space=pltpu.VMEM)] * (2 + count + 2 * held),
        out_specs=anywhere if final else [pl.BlockSpec(memory_space=pltpu.VMEM)] * 2,
        out_shape=jax.ShapeDtypeStruct((rows, width), jnp.bfloat16) if final else state_shapes,
        scratch_shapes=scratch,
        compiler_params=pltpu.CompilerParams(vmem_limit_bytes=24 * 2**20),
        cost_estimate=pl.CostEstimate(
            flops=4 * rows * width * span, bytes_accessed=4 * rows * width, transcendentals=heads * rows * span
        ),
    )(table, queries, *blocks, *(state if held else ()))


def ahead(block, distance):
    size = lax.axis_size("ctx")
    return lax.ppermute(block, "ctx", [(i, i + distance) for i in range(size - distance)])


def in_row(block, step):
    size = lax.axis_size("ctx")
    return lax.ppermute(block, "ctx", [(i, i // ROW * ROW + (i + step) % ROW) for i in range(size)])


def per_device(queries, keys, values, key_value_scales, doc_lengths):
    rows = queries.shape[0]
    groups = key_value_scales.shape[2]
    own, other = join(keys, values)
    column = lax.axis_index("ctx") % ROW
    fourth = ahead(own, 4)
    table, other = make_table(doc_lengths, key_value_scales, other, rows, groups, (0, 4, 2, 3, 1))
    second = ahead(other, 2)
    third = in_row(jnp.where(column == 0, own, fourth), ROW - 1)
    nearest = in_row(jnp.where(column < ROW - 1, own, fourth), 1)
    state = attend(table, queries, (own, fourth, second), (0, 1, 2), final=False)
    state = attend(table, queries, (third,), (3,), state=state, final=False)
    return attend(table, queries, (nearest,), (4,), state=state)


def solution(mesh):
    return jax.shard_map(
        per_device,
        mesh=mesh,
        in_specs=(
            P(("seq", "ctx"), None),
            P(("seq", "ctx"), None),
            P(("seq", "ctx"), None),
            P("seq", None, None),
            P("seq"),
        ),
        out_specs=P(("seq", "ctx"), None),
        check_vma=False,
    )
```

```python
import functools
import math

import jax
import jax.numpy as jnp
from jax import lax
from jax.experimental import pallas as pl
from jax.experimental.pallas import tpu as pltpu
from jax.sharding import PartitionSpec as P

SCALE_BLOCK = 32
HEAD = 128
LOW = -1e30
LAST = (((1,), (1,)), ((), ()))
EXTRA = 16
CHUNK = 8
ROW = 4


def join_kernel(keys, values, own, sems):
    half = keys.shape[1]
    copies = [
        pltpu.make_async_copy(source, own.at[:, pl.ds(at * half, half)], sems.at[at])
        for at, source in enumerate((keys, values))
    ]
    for copy in copies:
        copy.start()
    for copy in copies:
        copy.wait()


def join(keys, values):
    rows, half = keys.shape
    far = [pltpu.with_memory_space_constraint(x, pltpu.HBM) for x in (keys, values)]
    return pl.pallas_call(
        join_kernel,
        in_specs=[pl.BlockSpec(memory_space=pltpu.HBM)] * 2,
        out_specs=pl.BlockSpec(memory_space=pltpu.VMEM),
        out_shape=pltpu.VMEM((rows, 2 * half), keys.dtype),
        scratch_shapes=[pltpu.SemaphoreType.DMA((2,))],
        compiler_params=pltpu.CompilerParams(vmem_limit_bytes=4 * 2**20),
    )(*far)


def pick_kernel(own, far, to_left, to_right):
    column = lax.rem(lax.axis_index("ctx"), ROW)
    mine, other = own[...], far[...]
    to_left[...] = jnp.where(column == 0, mine, other)
    to_right[...] = jnp.where(column < ROW - 1, mine, other)


def pick(own, far):
    vmem = pl.BlockSpec(memory_space=pltpu.VMEM)
    return pl.pallas_call(
        pick_kernel,
        in_specs=[vmem] * 2,
        out_specs=[vmem] * 2,
        out_shape=[pltpu.VMEM(own.shape, own.dtype)] * 2,
        compiler_params=pltpu.CompilerParams(vmem_limit_bytes=4 * 2**20),
    )(own, far)


def setup_kernel(docs_far, scales_far, queries, table, near, docs, scales, sems, *, groups, rows, backs):
    pairs = ((docs_far, docs), (scales_far, scales), (queries, near))
    copies = [pltpu.make_async_copy(source, target, sems.at[at]) for at, (source, target) in enumerate(pairs)]
    for copy in copies:
        copy.start()
    copies[0].wait()
    copies[1].wait()
    first = lax.axis_index("ctx") * rows
    pieces = rows // SCALE_BLOCK
    qpos = first + lax.broadcasted_iota(jnp.int32, (8, rows), 1)

    def visit(doc, carry):
        end, start = carry
        end = end + docs[doc]
        return end, jnp.where(end <= qpos, end, start)

    _, start = lax.fori_loop(0, docs.shape[0], visit, (0, jnp.zeros((8, rows), jnp.int32)), unroll=8)
    both = jnp.concatenate([scales[0], scales[1]], axis=0)
    place = lax.broadcasted_iota(jnp.int32, both.shape, 1)
    lane = lax.broadcasted_iota(jnp.int32, (2 * groups, rows), 1) // SCALE_BLOCK
    upper = lax.broadcasted_iota(jnp.int32, (2 * groups, rows), 0) < groups
    for slot, back in enumerate(backs):
        kpos = first - back * rows + lax.broadcasted_iota(jnp.int32, (rows, rows), 0)
        keep = kpos >= start[:1]
        if back == 0:
            keep = keep & (kpos <= qpos[:1])
        table[slot, :rows, :] = jnp.where(keep, 0.0, LOW)
        line = jnp.ones((2 * groups, rows), jnp.float32)
        for piece in range(pieces):
            block = jnp.maximum(first // SCALE_BLOCK - back * pieces + piece, 0)
            column = jnp.sum(jnp.where(place == block, both, 0.0), axis=1, keepdims=True)
            wide = jnp.broadcast_to(column, (2 * groups, rows))
            at = rows + 2 * groups * piece
            table[slot, at : at + 2 * groups, :] = jnp.where(
                upper, wide * (math.log2(math.e) / math.sqrt(HEAD)), jnp.log2(wide)
            )
            line = jnp.where(lane == piece, wide, line)
        at = rows + 2 * groups * pieces
        table[slot, at : at + 2 * groups, :] = 1.0 / line
    copies[2].wait()


def setup(docs, scales, queries, groups, backs):
    rows = queries.shape[0]
    depth = rows + 2 * groups * (rows // SCALE_BLOCK + 1)
    scales = scales.transpose(1, 2, 0)
    far = [pltpu.with_memory_space_constraint(x, pltpu.HBM) for x in (docs, scales, queries)]
    return pl.pallas_call(
        functools.partial(setup_kernel, groups=groups, rows=rows, backs=backs),
        in_specs=[pl.BlockSpec(memory_space=pltpu.HBM)] * 3,
        out_specs=[pl.BlockSpec(memory_space=pltpu.VMEM)] * 2,
        out_shape=[
            pltpu.VMEM((len(backs), depth, rows), jnp.float32),
            pltpu.VMEM(queries.shape, queries.dtype),
        ],
        scratch_shapes=[
            pltpu.SMEM(docs.shape, docs.dtype),
            pltpu.VMEM(scales.shape, scales.dtype),
            pltpu.SemaphoreType.DMA((3,)),
        ],
        compiler_params=pltpu.CompilerParams(vmem_limit_bytes=4 * 2**20),
    )(*far)


def kernel(*refs, slots, groups, rows, state, final, chunk):
    count = len(slots)
    refs = list(refs)
    sources = refs[: 2 + count + 2 * state]
    refs = refs[len(sources) :]
    if final:
        out = refs[0]
        refs = refs[1:]
    else:
        acc_out, stat_out = refs[:2]
        refs = refs[2:]
    buffers = sources
    bias, kparts, vparts, scores, probs = refs[:5]
    if final:
        stage, out_sems = refs[5:]
    width = sources[1].shape[1]
    heads = width // HEAD
    per = heads // groups
    pieces = rows // SCALE_BLOCK

    table, queries, blocks = buffers[0], buffers[1], buffers[2 : 2 + count]
    if state:
        acc_in, stat_in = buffers[2 + count], buffers[3 + count]

    deep = lax.broadcasted_iota(jnp.int32, (EXTRA, rows), 0)

    def prepare(group):
        at = group % 3
        for slot in range(count):
            for piece in range(pieces):
                source = pl.ds(piece * SCALE_BLOCK, SCALE_BLOCK)
                target = pl.ds(slot * rows + piece * SCALE_BLOCK, SCALE_BLOCK)
                base = rows + 2 * groups * piece + group
                kscale = table[slots[slot], base : base + 1, :]
                scaled = blocks[slot][source, group * HEAD : (group + 1) * HEAD].astype(jnp.float32) * kscale
                high = scaled.astype(jnp.bfloat16)
                kparts[at, target, :HEAD] = high
                kparts[at, target, HEAD:] = (scaled - high.astype(jnp.float32)).astype(jnp.bfloat16)
                bias[at, target, :] = table[slots[slot], source, :] + table[slots[slot], base + groups : base + groups + 1, :]
            base = rows + 2 * groups * pieces + groups + group
            inverse = table[slots[slot], base : base + 1, :]
            high = inverse.astype(jnp.bfloat16).astype(jnp.float32)
            ones = jnp.where(deep == 0, high, jnp.where(deep == 1, inverse - high, 0.0))
            columns = pl.ds(slot * rows, rows)
            vparts[at, :HEAD, columns] = blocks[slot][:, (groups + group) * HEAD : (groups + group + 1) * HEAD].T
            vparts[at, HEAD:, columns] = ones.astype(jnp.bfloat16)

    steps = heads // chunk
    tops = {}

    def some(step):
        return range(step * chunk, (step + 1) * chunk)

    def across(ref, offset, step):
        return jnp.concatenate([ref[offset + h : offset + h + 1, :] for h in some(step)], axis=1)

    def score_part(step):
        group = step * chunk // per
        if step * chunk % per == 0:
            prepare(group)
        query = jnp.concatenate([queries[:, h * HEAD : (h + 1) * HEAD] for h in some(step)], axis=0)
        query = jnp.concatenate([query, query], axis=1)
        score = lax.dot_general(kparts[group % 3], query, LAST, preferred_element_type=jnp.float32)
        score = score + jnp.concatenate([bias[group % 3]] * chunk, axis=1)
        scores[step % 2] = score
        top = jnp.max(score, axis=0, keepdims=True)
        if state:
            top = jnp.maximum(top, across(stat_in, 0, step))
        tops[step] = top

    def prob_part(step):
        probs[step % 2] = jnp.exp2(scores[step % 2] - tops[step]).astype(jnp.bfloat16)

    def send(group):
        columns = pl.ds(group * per * HEAD, per * HEAD)
        return pltpu.make_async_copy(stage.at[:, columns], out.at[:, columns], out_sems.at[group])

    def value_part(step):
        group = step * chunk // per
        both = jnp.dot(vparts[group % 3], probs[step % 2], preferred_element_type=jnp.float32)
        total = both[HEAD : HEAD + 1] + both[HEAD + 1 : HEAD + 2]
        result = both[:HEAD]
        if state:
            keep = jnp.exp2(across(stat_in, 0, step) - tops[step])
            total = total + keep * across(stat_in, heads, step)
            old = jnp.concatenate([acc_in[h * HEAD : (h + 1) * HEAD, :] for h in some(step)], axis=1)
            result = result + keep * old
        if final:
            result = result * (1.0 / total)
        for at, h in enumerate(some(step)):
            lanes = slice(at * rows, (at + 1) * rows)
            if final:
                stage[:, h * HEAD : (h + 1) * HEAD] = result[:, lanes].T.astype(jnp.bfloat16)
            else:
                acc_out[h * HEAD : (h + 1) * HEAD, :] = result[:, lanes]
                stat_out[h : h + 1, :] = tops[step][:, lanes]
                stat_out[heads + h : heads + h + 1, :] = total[:, lanes]
        if final and (step + 1) * chunk % per == 0:
            send(group).start()

    for step in range(steps + 2):
        if step < steps:
            score_part(step)
        if 1 <= step <= steps:
            prob_part(step - 1)
        if 2 <= step:
            value_part(step - 2)
    if final:
        for group in range(groups):
            send(group).wait()


def attend(table, queries, blocks, groups, slots, state=None, final=True, chunk=CHUNK):
    rows, width = queries.shape
    count = len(slots)
    span = count * rows
    heads = width // HEAD
    anywhere = pl.BlockSpec(memory_space=pl.ANY)
    state_shapes = [
        jax.ShapeDtypeStruct((width, rows), jnp.float32),
        jax.ShapeDtypeStruct((2 * heads, rows), jnp.float32),
    ]
    held = state is not None
    scratch = []
    scratch += [
        pltpu.VMEM((3, span, rows), jnp.float32),
        pltpu.VMEM((3, span, 2 * HEAD), jnp.bfloat16),
        pltpu.VMEM((3, HEAD + EXTRA, span), jnp.bfloat16),
        pltpu.VMEM((2, span, chunk * rows), jnp.float32),
        pltpu.VMEM((2, span, chunk * rows), jnp.bfloat16),
    ]
    if final:
        scratch += [pltpu.VMEM((rows, width), jnp.bfloat16), pltpu.SemaphoreType.DMA((groups,))]
    return pl.pallas_call(
        functools.partial(kernel, slots=slots, groups=groups, rows=rows, state=held, final=final, chunk=chunk),
        in_specs=[pl.BlockSpec(memory_space=pltpu.VMEM)] * (2 + count + 2 * held),
        out_specs=anywhere if final else [pl.BlockSpec(memory_space=pltpu.VMEM)] * 2,
        out_shape=jax.ShapeDtypeStruct((rows, width), jnp.bfloat16) if final else state_shapes,
        scratch_shapes=scratch,
        compiler_params=pltpu.CompilerParams(vmem_limit_bytes=24 * 2**20),
        cost_estimate=pl.CostEstimate(
            flops=4 * rows * width * span, bytes_accessed=4 * rows * width, transcendentals=heads * rows * span
        ),
    )(table, queries, *blocks, *(state if held else ()))


def ahead(block, distance):
    size = lax.axis_size("ctx")
    return lax.ppermute(block, "ctx", [(i, i + distance) for i in range(size - distance)])


def in_row(block, step):
    size = lax.axis_size("ctx")
    return lax.ppermute(block, "ctx", [(i, i // ROW * ROW + (i + step) % ROW) for i in range(size)])


def per_device(queries, keys, values, key_value_scales, doc_lengths):
    groups = key_value_scales.shape[2]
    own = join(keys, values)
    fourth = ahead(own, 4)
    second = ahead(own, 2)
    to_left, to_right = pick(own, fourth)
    nearest = in_row(to_right, 1)
    third = in_row(to_left, ROW - 1)
    table, near = setup(doc_lengths, key_value_scales, queries, groups, (0, 4, 2, 1, 3))
    state = attend(table, near, (own, fourth, second), groups, (0, 1, 2), final=False)
    state = attend(table, near, (nearest,), groups, (3,), state=state, final=False)
    return attend(table, near, (third,), groups, (4,), state=state)


def solution(mesh):
    return jax.shard_map(
        per_device,
        mesh=mesh,
        in_specs=(
            P(("seq", "ctx"), None),
            P(("seq", "ctx"), None),
            P(("seq", "ctx"), None),
            P("seq", None, None),
            P("seq"),
        ),
        out_specs=P(("seq", "ctx"), None),
        check_vma=False,
    )
```

```python
import functools
import math

import jax
import jax.numpy as jnp
from jax import lax
from jax.experimental import pallas as pl
from jax.experimental.pallas import tpu as pltpu
from jax.sharding import PartitionSpec as P

SCALE_BLOCK = 32
HEAD = 128
LOW = -1e30
LAST = (((1,), (1,)), ((), ()))
EXTRA = 16
CHUNK = 8
ROW = 4


def join_kernel(keys, values, own, sems):
    half = keys.shape[1]
    copies = [
        pltpu.make_async_copy(source, own.at[:, pl.ds(at * half, half)], sems.at[at])
        for at, source in enumerate((keys, values))
    ]
    for copy in copies:
        copy.start()
    for copy in copies:
        copy.wait()


def join(keys, values):
    rows, half = keys.shape
    far = [pltpu.with_memory_space_constraint(x, pltpu.HBM) for x in (keys, values)]
    return pl.pallas_call(
        join_kernel,
        in_specs=[pl.BlockSpec(memory_space=pltpu.HBM)] * 2,
        out_specs=pl.BlockSpec(memory_space=pltpu.VMEM),
        out_shape=pltpu.VMEM((rows, 2 * half), keys.dtype),
        scratch_shapes=[pltpu.SemaphoreType.DMA((2,))],
        compiler_params=pltpu.CompilerParams(vmem_limit_bytes=4 * 2**20),
    )(*far)


def pick_kernel(own, far, inner, outer):
    column = lax.rem(lax.axis_index("ctx"), ROW)
    mine, other = own[...], far[...]
    inner[...] = jnp.where(lax.rem(column, 2) == 0, mine, other)
    outer[...] = jnp.where(column < 2, mine, other)


def pick(own, far):
    vmem = pl.BlockSpec(memory_space=pltpu.VMEM)
    return pl.pallas_call(
        pick_kernel,
        in_specs=[vmem] * 2,
        out_specs=[vmem] * 2,
        out_shape=[pltpu.VMEM(own.shape, own.dtype)] * 2,
        compiler_params=pltpu.CompilerParams(vmem_limit_bytes=4 * 2**20),
    )(own, far)


def setup_kernel(docs_far, scales_far, queries, table, near, docs, scales, sems, *, groups, rows, backs):
    pairs = ((docs_far, docs), (scales_far, scales), (queries, near))
    copies = [pltpu.make_async_copy(source, target, sems.at[at]) for at, (source, target) in enumerate(pairs)]
    for copy in copies:
        copy.start()
    copies[0].wait()
    copies[1].wait()
    first = lax.axis_index("ctx") * rows
    pieces = rows // SCALE_BLOCK
    qpos = first + lax.broadcasted_iota(jnp.int32, (8, rows), 1)

    def visit(doc, carry):
        end, start = carry
        end = end + docs[doc]
        return end, jnp.where(end <= qpos, end, start)

    _, start = lax.fori_loop(0, docs.shape[0], visit, (0, jnp.zeros((8, rows), jnp.int32)), unroll=8)
    both = jnp.concatenate([scales[0], scales[1]], axis=0)
    place = lax.broadcasted_iota(jnp.int32, both.shape, 1)
    lane = lax.broadcasted_iota(jnp.int32, (2 * groups, rows), 1) // SCALE_BLOCK
    upper = lax.broadcasted_iota(jnp.int32, (2 * groups, rows), 0) < groups
    even = lax.rem(lax.axis_index("ctx"), 2) == 0
    for slot, (back, odd_back) in enumerate(backs):
        if back != odd_back:
            back = jnp.where(even, back, odd_back)
        kpos = first - back * rows + lax.broadcasted_iota(jnp.int32, (rows, rows), 0)
        keep = kpos >= start[:1]
        if slot == 0:
            keep = keep & (kpos <= qpos[:1])
        table[slot, :rows, :] = jnp.where(keep, 0.0, LOW)
        line = jnp.ones((2 * groups, rows), jnp.float32)
        for piece in range(pieces):
            block = jnp.maximum(first // SCALE_BLOCK - back * pieces + piece, 0)
            column = jnp.sum(jnp.where(place == block, both, 0.0), axis=1, keepdims=True)
            wide = jnp.broadcast_to(column, (2 * groups, rows))
            at = rows + 2 * groups * piece
            table[slot, at : at + 2 * groups, :] = jnp.where(
                upper, wide * (math.log2(math.e) / math.sqrt(HEAD)), jnp.log2(wide)
            )
            line = jnp.where(lane == piece, wide, line)
        at = rows + 2 * groups * pieces
        table[slot, at : at + 2 * groups, :] = 1.0 / line
    copies[2].wait()


def setup(docs, scales, queries, groups, backs):
    rows = queries.shape[0]
    depth = rows + 2 * groups * (rows // SCALE_BLOCK + 1)
    scales = scales.transpose(1, 2, 0)
    far = [pltpu.with_memory_space_constraint(x, pltpu.HBM) for x in (docs, scales, queries)]
    return pl.pallas_call(
        functools.partial(setup_kernel, groups=groups, rows=rows, backs=backs),
        in_specs=[pl.BlockSpec(memory_space=pltpu.HBM)] * 3,
        out_specs=[pl.BlockSpec(memory_space=pltpu.VMEM)] * 2,
        out_shape=[
            pltpu.VMEM((len(backs), depth, rows), jnp.float32),
            pltpu.VMEM(queries.shape, queries.dtype),
        ],
        scratch_shapes=[
            pltpu.SMEM(docs.shape, docs.dtype),
            pltpu.VMEM(scales.shape, scales.dtype),
            pltpu.SemaphoreType.DMA((3,)),
        ],
        compiler_params=pltpu.CompilerParams(vmem_limit_bytes=4 * 2**20),
    )(*far)


def kernel(*refs, slots, groups, rows, state, final, chunk):
    count = len(slots)
    refs = list(refs)
    sources = refs[: 2 + count + 2 * state]
    refs = refs[len(sources) :]
    if final:
        out = refs[0]
        refs = refs[1:]
    else:
        acc_out, stat_out = refs[:2]
        refs = refs[2:]
    buffers = sources
    bias, kparts, vparts, scores, probs = refs[:5]
    if final:
        stage, out_sems = refs[5:]
    width = sources[1].shape[1]
    heads = width // HEAD
    per = heads // groups
    pieces = rows // SCALE_BLOCK

    table, queries, blocks = buffers[0], buffers[1], buffers[2 : 2 + count]
    if state:
        acc_in, stat_in = buffers[2 + count], buffers[3 + count]

    deep = lax.broadcasted_iota(jnp.int32, (EXTRA, rows), 0)

    def prepare(group):
        at = group % 3
        for slot in range(count):
            for piece in range(pieces):
                source = pl.ds(piece * SCALE_BLOCK, SCALE_BLOCK)
                target = pl.ds(slot * rows + piece * SCALE_BLOCK, SCALE_BLOCK)
                base = rows + 2 * groups * piece + group
                kscale = table[slots[slot], base : base + 1, :]
                scaled = blocks[slot][source, group * HEAD : (group + 1) * HEAD].astype(jnp.float32) * kscale
                high = scaled.astype(jnp.bfloat16)
                kparts[at, target, :HEAD] = high
                kparts[at, target, HEAD:] = (scaled - high.astype(jnp.float32)).astype(jnp.bfloat16)
                bias[at, target, :] = table[slots[slot], source, :] + table[slots[slot], base + groups : base + groups + 1, :]
            base = rows + 2 * groups * pieces + groups + group
            inverse = table[slots[slot], base : base + 1, :]
            high = inverse.astype(jnp.bfloat16).astype(jnp.float32)
            ones = jnp.where(deep == 0, high, jnp.where(deep == 1, inverse - high, 0.0))
            columns = pl.ds(slot * rows, rows)
            vparts[at, :HEAD, columns] = blocks[slot][:, (groups + group) * HEAD : (groups + group + 1) * HEAD].T
            vparts[at, HEAD:, columns] = ones.astype(jnp.bfloat16)

    steps = heads // chunk
    tops = {}

    def some(step):
        return range(step * chunk, (step + 1) * chunk)

    def across(ref, offset, step):
        return jnp.concatenate([ref[offset + h : offset + h + 1, :] for h in some(step)], axis=1)

    def score_part(step):
        group = step * chunk // per
        if step * chunk % per == 0:
            prepare(group)
        query = jnp.concatenate([queries[:, h * HEAD : (h + 1) * HEAD] for h in some(step)], axis=0)
        query = jnp.concatenate([query, query], axis=1)
        score = lax.dot_general(kparts[group % 3], query, LAST, preferred_element_type=jnp.float32)
        score = score + jnp.concatenate([bias[group % 3]] * chunk, axis=1)
        scores[step % 2] = score
        top = jnp.max(score, axis=0, keepdims=True)
        if state:
            top = jnp.maximum(top, across(stat_in, 0, step))
        tops[step] = top

    def prob_part(step):
        probs[step % 2] = jnp.exp2(scores[step % 2] - tops[step]).astype(jnp.bfloat16)

    def send(group):
        columns = pl.ds(group * per * HEAD, per * HEAD)
        return pltpu.make_async_copy(stage.at[:, columns], out.at[:, columns], out_sems.at[group])

    def value_part(step):
        group = step * chunk // per
        both = jnp.dot(vparts[group % 3], probs[step % 2], preferred_element_type=jnp.float32)
        total = both[HEAD : HEAD + 1] + both[HEAD + 1 : HEAD + 2]
        result = both[:HEAD]
        if state:
            keep = jnp.exp2(across(stat_in, 0, step) - tops[step])
            total = total + keep * across(stat_in, heads, step)
            old = jnp.concatenate([acc_in[h * HEAD : (h + 1) * HEAD, :] for h in some(step)], axis=1)
            result = result + keep * old
        if final:
            result = result * (1.0 / total)
        for at, h in enumerate(some(step)):
            lanes = slice(at * rows, (at + 1) * rows)
            if final:
                stage[:, h * HEAD : (h + 1) * HEAD] = result[:, lanes].T.astype(jnp.bfloat16)
            else:
                acc_out[h * HEAD : (h + 1) * HEAD, :] = result[:, lanes]
                stat_out[h : h + 1, :] = tops[step][:, lanes]
                stat_out[heads + h : heads + h + 1, :] = total[:, lanes]
        if final and (step + 1) * chunk % per == 0:
            send(group).start()

    for step in range(steps + 2):
        if step < steps:
            score_part(step)
        if 1 <= step <= steps:
            prob_part(step - 1)
        if 2 <= step:
            value_part(step - 2)
    if final:
        for group in range(groups):
            send(group).wait()


def attend(table, queries, blocks, groups, slots, state=None, final=True, chunk=CHUNK):
    rows, width = queries.shape
    count = len(slots)
    span = count * rows
    heads = width // HEAD
    anywhere = pl.BlockSpec(memory_space=pl.ANY)
    state_shapes = [
        jax.ShapeDtypeStruct((width, rows), jnp.float32),
        jax.ShapeDtypeStruct((2 * heads, rows), jnp.float32),
    ]
    held = state is not None
    scratch = []
    scratch += [
        pltpu.VMEM((3, span, rows), jnp.float32),
        pltpu.VMEM((3, span, 2 * HEAD), jnp.bfloat16),
        pltpu.VMEM((3, HEAD + EXTRA, span), jnp.bfloat16),
        pltpu.VMEM((2, span, chunk * rows), jnp.float32),
        pltpu.VMEM((2, span, chunk * rows), jnp.bfloat16),
    ]
    if final:
        scratch += [pltpu.VMEM((rows, width), jnp.bfloat16), pltpu.SemaphoreType.DMA((groups,))]
    return pl.pallas_call(
        functools.partial(kernel, slots=slots, groups=groups, rows=rows, state=held, final=final, chunk=chunk),
        in_specs=[pl.BlockSpec(memory_space=pltpu.VMEM)] * (2 + count + 2 * held),
        out_specs=anywhere if final else [pl.BlockSpec(memory_space=pltpu.VMEM)] * 2,
        out_shape=jax.ShapeDtypeStruct((rows, width), jnp.bfloat16) if final else state_shapes,
        scratch_shapes=scratch,
        compiler_params=pltpu.CompilerParams(vmem_limit_bytes=24 * 2**20),
        cost_estimate=pl.CostEstimate(
            flops=4 * rows * width * span, bytes_accessed=4 * rows * width, transcendentals=heads * rows * span
        ),
    )(table, queries, *blocks, *(state if held else ()))


def ahead(block, distance):
    size = lax.axis_size("ctx")
    return lax.ppermute(block, "ctx", [(i, i + distance) for i in range(size - distance)])


def in_row(block, places):
    size = lax.axis_size("ctx")
    return lax.ppermute(block, "ctx", [(i, i // ROW * ROW + places[i % ROW]) for i in range(size)])


def per_device(queries, keys, values, key_value_scales, doc_lengths):
    groups = key_value_scales.shape[2]
    own = join(keys, values)
    fourth = ahead(own, 4)
    second = ahead(own, 2)
    inner, outer = pick(own, fourth)
    inner = in_row(inner, (1, 0, 3, 2))
    outer = in_row(outer, (3, 2, 1, 0))
    backs = ((0, 0), (4, 4), (2, 2), (3, 1), (1, 3))
    table, near = setup(doc_lengths, key_value_scales, queries, groups, backs)
    state = attend(table, near, (own, fourth, second), groups, (0, 1, 2), final=False)
    state = attend(table, near, (inner,), groups, (3,), state=state, final=False)
    return attend(table, near, (outer,), groups, (4,), state=state)


def solution(mesh):
    return jax.shard_map(
        per_device,
        mesh=mesh,
        in_specs=(
            P(("seq", "ctx"), None),
            P(("seq", "ctx"), None),
            P(("seq", "ctx"), None),
            P("seq", None, None),
            P("seq"),
        ),
        out_specs=P(("seq", "ctx"), None),
        check_vma=False,
    )
```

```python
import functools
import math

import jax
import jax.numpy as jnp
from jax import lax
from jax.experimental import pallas as pl
from jax.experimental.pallas import tpu as pltpu
from jax.sharding import PartitionSpec as P

SCALE_BLOCK = 32
HEAD = 128
LOW = -1e30
LAST = (((1,), (1,)), ((), ()))
EXTRA = 16
CHUNK = 8
ROW = 4


def join_kernel(keys, values, own, sems):
    half = keys.shape[1]
    copies = [
        pltpu.make_async_copy(source, own.at[:, pl.ds(at * half, half)], sems.at[at])
        for at, source in enumerate((keys, values))
    ]
    for copy in copies:
        copy.start()
    for copy in copies:
        copy.wait()


def join(keys, values):
    rows, half = keys.shape
    far = [pltpu.with_memory_space_constraint(x, pltpu.HBM) for x in (keys, values)]
    return pl.pallas_call(
        join_kernel,
        in_specs=[pl.BlockSpec(memory_space=pltpu.HBM)] * 2,
        out_specs=pl.BlockSpec(memory_space=pltpu.VMEM),
        out_shape=pltpu.VMEM((rows, 2 * half), keys.dtype),
        scratch_shapes=[pltpu.SemaphoreType.DMA((2,))],
        compiler_params=pltpu.CompilerParams(vmem_limit_bytes=4 * 2**20),
    )(*far)


def pick_kernel(own, far, inner, outer):
    column = lax.rem(lax.axis_index("ctx"), ROW)
    mine, other = own[...], far[...]
    inner[...] = jnp.where(lax.rem(column, 2) == 0, mine, other)
    outer[...] = jnp.where(column < 2, mine, other)


def pick(own, far):
    vmem = pl.BlockSpec(memory_space=pltpu.VMEM)
    return pl.pallas_call(
        pick_kernel,
        in_specs=[vmem] * 2,
        out_specs=[vmem] * 2,
        out_shape=[pltpu.VMEM(own.shape, own.dtype)] * 2,
        compiler_params=pltpu.CompilerParams(vmem_limit_bytes=4 * 2**20),
    )(own, far)


def setup_kernel(docs_far, scales_far, queries, table, near, docs, scales, sems, *, groups, rows, backs):
    pairs = ((docs_far, docs), (scales_far, scales), (queries, near))
    copies = [pltpu.make_async_copy(source, target, sems.at[at]) for at, (source, target) in enumerate(pairs)]
    for copy in copies:
        copy.start()
    copies[0].wait()
    copies[1].wait()
    first = lax.axis_index("ctx") * rows
    pieces = rows // SCALE_BLOCK
    qpos = first + lax.broadcasted_iota(jnp.int32, (8, rows), 1)

    def visit(doc, carry):
        end, start = carry
        end = end + docs[doc]
        return end, jnp.where(end <= qpos, end, start)

    _, start = lax.fori_loop(0, docs.shape[0], visit, (0, jnp.zeros((8, rows), jnp.int32)), unroll=8)
    both = jnp.concatenate([scales[0], scales[1]], axis=0)
    place = lax.broadcasted_iota(jnp.int32, both.shape, 1)
    lane = lax.broadcasted_iota(jnp.int32, (2 * groups, rows), 1) // SCALE_BLOCK
    upper = lax.broadcasted_iota(jnp.int32, (2 * groups, rows), 0) < groups
    even = lax.rem(lax.axis_index("ctx"), 2) == 0
    for slot, (back, odd_back) in enumerate(backs):
        if back != odd_back:
            back = jnp.where(even, back, odd_back)
        kpos = first - back * rows + lax.broadcasted_iota(jnp.int32, (rows, rows), 0)
        keep = kpos >= start[:1]
        if slot == 0:
            keep = keep & (kpos <= qpos[:1])
        table[slot, :rows, :] = jnp.where(keep, 0.0, LOW)
        line = jnp.ones((2 * groups, rows), jnp.float32)
        for piece in range(pieces):
            block = jnp.maximum(first // SCALE_BLOCK - back * pieces + piece, 0)
            column = jnp.sum(jnp.where(place == block, both, 0.0), axis=1, keepdims=True)
            wide = jnp.broadcast_to(column, (2 * groups, rows))
            at = rows + 2 * groups * piece
            table[slot, at : at + 2 * groups, :] = jnp.where(
                upper, wide * (math.log2(math.e) / math.sqrt(HEAD)), jnp.log2(wide)
            )
            line = jnp.where(lane == piece, wide, line)
        at = rows + 2 * groups * pieces
        table[slot, at : at + 2 * groups, :] = 1.0 / line
    copies[2].wait()


def setup(docs, scales, queries, groups, backs):
    rows = queries.shape[0]
    depth = rows + 2 * groups * (rows // SCALE_BLOCK + 1)
    scales = scales.transpose(1, 2, 0)
    far = [pltpu.with_memory_space_constraint(x, pltpu.HBM) for x in (docs, scales, queries)]
    return pl.pallas_call(
        functools.partial(setup_kernel, groups=groups, rows=rows, backs=backs),
        in_specs=[pl.BlockSpec(memory_space=pltpu.HBM)] * 3,
        out_specs=[pl.BlockSpec(memory_space=pltpu.VMEM)] * 2,
        out_shape=[
            pltpu.VMEM((len(backs), depth, rows), jnp.float32),
            pltpu.VMEM(queries.shape, queries.dtype),
        ],
        scratch_shapes=[
            pltpu.SMEM(docs.shape, docs.dtype),
            pltpu.VMEM(scales.shape, scales.dtype),
            pltpu.SemaphoreType.DMA((3,)),
        ],
        compiler_params=pltpu.CompilerParams(vmem_limit_bytes=4 * 2**20),
    )(*far)


def kernel(*refs, slots, groups, rows, state, final, chunk):
    count = len(slots)
    refs = list(refs)
    sources = refs[: 2 + count + 2 * state]
    refs = refs[len(sources) :]
    if final:
        out = refs[0]
        refs = refs[1:]
    else:
        acc_out, stat_out = refs[:2]
        refs = refs[2:]
    buffers = sources
    bias, kparts, vparts, scores, probs = refs[:5]
    if final:
        stage, out_sems = refs[5:]
    width = sources[1].shape[1]
    heads = width // HEAD
    per = heads // groups
    pieces = rows // SCALE_BLOCK

    table, queries, blocks = buffers[0], buffers[1], buffers[2 : 2 + count]
    if state:
        acc_in, stat_in = buffers[2 + count], buffers[3 + count]

    deep = lax.broadcasted_iota(jnp.int32, (EXTRA, rows), 0)

    def prepare(group):
        at = group % 3
        for slot in range(count):
            for piece in range(pieces):
                source = pl.ds(piece * SCALE_BLOCK, SCALE_BLOCK)
                target = pl.ds(slot * rows + piece * SCALE_BLOCK, SCALE_BLOCK)
                base = rows + 2 * groups * piece + group
                bias[at, target, :] = table[slots[slot], source, :] + table[slots[slot], base + groups : base + groups + 1, :]
            base = rows + 2 * groups * pieces + groups + group
            inverse = table[slots[slot], base : base + 1, :]
            high = inverse.astype(jnp.bfloat16).astype(jnp.float32)
            ones = jnp.where(deep == 0, high, jnp.where(deep == 1, inverse - high, 0.0))
            columns = pl.ds(slot * rows, rows)
            kparts[at, columns, :] = blocks[slot][:, group * HEAD : (group + 1) * HEAD]
            vparts[at, :HEAD, columns] = blocks[slot][:, (groups + group) * HEAD : (groups + group + 1) * HEAD].T
            vparts[at, HEAD:, columns] = ones.astype(jnp.bfloat16)

    steps = heads // chunk
    tops = {}

    def some(step):
        return range(step * chunk, (step + 1) * chunk)

    def across(ref, offset, step):
        return jnp.concatenate([ref[offset + h : offset + h + 1, :] for h in some(step)], axis=1)

    def score_part(step):
        group = step * chunk // per
        if step * chunk % per == 0:
            prepare(group)
        query = jnp.concatenate([queries[:, h * HEAD : (h + 1) * HEAD] for h in some(step)], axis=0)
        score = lax.dot_general(kparts[group % 3], query, LAST, preferred_element_type=jnp.float32)
        scaled = []
        for at in range(count * pieces):
            base = rows + 2 * groups * (at % pieces) + group
            kscale = jnp.concatenate([table[slots[at // pieces], base : base + 1, :]] * chunk, axis=1)
            keys = slice(at * SCALE_BLOCK, (at + 1) * SCALE_BLOCK)
            scaled.append(score[keys] * kscale + jnp.concatenate([bias[group % 3, keys, :]] * chunk, axis=1))
        score = jnp.concatenate(scaled, axis=0)
        scores[step % 2] = score
        top = jnp.max(score, axis=0, keepdims=True)
        if state:
            top = jnp.maximum(top, across(stat_in, 0, step))
        tops[step] = top

    def prob_part(step):
        probs[step % 2] = jnp.exp2(scores[step % 2] - tops[step]).astype(jnp.bfloat16)

    def send(group):
        columns = pl.ds(group * per * HEAD, per * HEAD)
        return pltpu.make_async_copy(stage.at[:, columns], out.at[:, columns], out_sems.at[group])

    def value_part(step):
        group = step * chunk // per
        both = jnp.dot(vparts[group % 3], probs[step % 2], preferred_element_type=jnp.float32)
        total = both[HEAD : HEAD + 1] + both[HEAD + 1 : HEAD + 2]
        result = both[:HEAD]
        if state:
            keep = jnp.exp2(across(stat_in, 0, step) - tops[step])
            total = total + keep * across(stat_in, heads, step)
            old = jnp.concatenate([acc_in[h * HEAD : (h + 1) * HEAD, :] for h in some(step)], axis=1)
            result = result + keep * old
        if final:
            result = result * (1.0 / total)
        for at, h in enumerate(some(step)):
            lanes = slice(at * rows, (at + 1) * rows)
            if final:
                stage[:, h * HEAD : (h + 1) * HEAD] = result[:, lanes].astype(jnp.bfloat16).T
            else:
                acc_out[h * HEAD : (h + 1) * HEAD, :] = result[:, lanes]
                stat_out[h : h + 1, :] = tops[step][:, lanes]
                stat_out[heads + h : heads + h + 1, :] = total[:, lanes]
        if final and (step + 1) * chunk % per == 0:
            send(group).start()

    for step in range(steps + 2):
        if step < steps:
            score_part(step)
        if 1 <= step <= steps:
            prob_part(step - 1)
        if 2 <= step:
            value_part(step - 2)
    if final:
        for group in range(groups):
            send(group).wait()


def attend(table, queries, blocks, groups, slots, state=None, final=True, chunk=CHUNK):
    rows, width = queries.shape
    count = len(slots)
    span = count * rows
    heads = width // HEAD
    anywhere = pl.BlockSpec(memory_space=pl.ANY)
    state_shapes = [
        jax.ShapeDtypeStruct((width, rows), jnp.float32),
        jax.ShapeDtypeStruct((2 * heads, rows), jnp.float32),
    ]
    held = state is not None
    scratch = []
    scratch += [
        pltpu.VMEM((3, span, rows), jnp.float32),
        pltpu.VMEM((3, span, HEAD), jnp.bfloat16),
        pltpu.VMEM((3, HEAD + EXTRA, span), jnp.bfloat16),
        pltpu.VMEM((2, span, chunk * rows), jnp.float32),
        pltpu.VMEM((2, span, chunk * rows), jnp.bfloat16),
    ]
    if final:
        scratch += [pltpu.VMEM((rows, width), jnp.bfloat16), pltpu.SemaphoreType.DMA((groups,))]
    return pl.pallas_call(
        functools.partial(kernel, slots=slots, groups=groups, rows=rows, state=held, final=final, chunk=chunk),
        in_specs=[pl.BlockSpec(memory_space=pltpu.VMEM)] * (2 + count + 2 * held),
        out_specs=anywhere if final else [pl.BlockSpec(memory_space=pltpu.VMEM)] * 2,
        out_shape=jax.ShapeDtypeStruct((rows, width), jnp.bfloat16) if final else state_shapes,
        scratch_shapes=scratch,
        compiler_params=pltpu.CompilerParams(vmem_limit_bytes=24 * 2**20),
        cost_estimate=pl.CostEstimate(
            flops=4 * rows * width * span, bytes_accessed=4 * rows * width, transcendentals=heads * rows * span
        ),
    )(table, queries, *blocks, *(state if held else ()))


def ahead(block, distance):
    size = lax.axis_size("ctx")
    return lax.ppermute(block, "ctx", [(i, i + distance) for i in range(size - distance)])


def in_row(block, places):
    size = lax.axis_size("ctx")
    return lax.ppermute(block, "ctx", [(i, i // ROW * ROW + places[i % ROW]) for i in range(size)])


def per_device(queries, keys, values, key_value_scales, doc_lengths):
    groups = key_value_scales.shape[2]
    own = join(keys, values)
    fourth = ahead(own, 4)
    second = ahead(own, 2)
    inner, outer = pick(own, fourth)
    inner = in_row(inner, (1, 0, 3, 2))
    outer = in_row(outer, (3, 2, 1, 0))
    backs = ((0, 0), (4, 4), (2, 2), (3, 1), (1, 3))
    table, near = setup(doc_lengths, key_value_scales, queries, groups, backs)
    state = attend(table, near, (own, fourth, second), groups, (0, 1, 2), final=False)
    state = attend(table, near, (inner,), groups, (3,), state=state, final=False)
    return attend(table, near, (outer,), groups, (4,), state=state)


def solution(mesh):
    return jax.shard_map(
        per_device,
        mesh=mesh,
        in_specs=(
            P(("seq", "ctx"), None),
            P(("seq", "ctx"), None),
            P(("seq", "ctx"), None),
            P("seq", None, None),
            P("seq"),
        ),
        out_specs=P(("seq", "ctx"), None),
        check_vma=False,
    )
```

```python
import functools
import math

import jax
import jax.numpy as jnp
from jax import lax
from jax.experimental import pallas as pl
from jax.experimental.pallas import tpu as pltpu
from jax.sharding import PartitionSpec as P

SCALE_BLOCK = 32
HEAD = 128
LOW = -1e30
LAST = (((1,), (1,)), ((), ()))
EXTRA = 16
CHUNK = 8
ROW = 4


def join_kernel(keys, values, own, sems):
    half = keys.shape[1]
    copies = [
        pltpu.make_async_copy(source, own.at[:, pl.ds(at * half, half)], sems.at[at])
        for at, source in enumerate((keys, values))
    ]
    for copy in copies:
        copy.start()
    for copy in copies:
        copy.wait()


def join(keys, values):
    rows, half = keys.shape
    far = [pltpu.with_memory_space_constraint(x, pltpu.HBM) for x in (keys, values)]
    return pl.pallas_call(
        join_kernel,
        in_specs=[pl.BlockSpec(memory_space=pltpu.HBM)] * 2,
        out_specs=pl.BlockSpec(memory_space=pltpu.VMEM),
        out_shape=pltpu.VMEM((rows, 2 * half), keys.dtype),
        scratch_shapes=[pltpu.SemaphoreType.DMA((2,))],
        compiler_params=pltpu.CompilerParams(vmem_limit_bytes=4 * 2**20),
    )(*far)


def pick_kernel(own, far, inner, outer):
    column = lax.rem(lax.axis_index("ctx"), ROW)
    mine, other = own[...], far[...]
    inner[...] = jnp.where(lax.rem(column, 2) == 0, mine, other)
    outer[...] = jnp.where(column < 2, mine, other)


def pick(own, far):
    vmem = pl.BlockSpec(memory_space=pltpu.VMEM)
    return pl.pallas_call(
        pick_kernel,
        in_specs=[vmem] * 2,
        out_specs=[vmem] * 2,
        out_shape=[pltpu.VMEM(own.shape, own.dtype)] * 2,
        compiler_params=pltpu.CompilerParams(vmem_limit_bytes=4 * 2**20),
    )(own, far)


def setup_kernel(docs_far, scales_far, queries, own, table, near, again, docs, scales, sems, *, groups, rows, backs):
    pairs = ((docs_far, docs), (scales_far, scales), (own, again), (queries, near))
    copies = [pltpu.make_async_copy(source, target, sems.at[at]) for at, (source, target) in enumerate(pairs)]
    for copy in copies:
        copy.start()
    copies[0].wait()
    copies[1].wait()
    first = lax.axis_index("ctx") * rows
    pieces = rows // SCALE_BLOCK
    qpos = first + lax.broadcasted_iota(jnp.int32, (8, rows), 1)

    def visit(doc, carry):
        end, start = carry
        end = end + docs[doc]
        return end, jnp.where(end <= qpos, end, start)

    _, start = lax.fori_loop(0, docs.shape[0], visit, (0, jnp.zeros((8, rows), jnp.int32)), unroll=8)
    both = jnp.concatenate([scales[0], scales[1]], axis=0)
    place = lax.broadcasted_iota(jnp.int32, both.shape, 1)
    lane = lax.broadcasted_iota(jnp.int32, (2 * groups, rows), 1) // SCALE_BLOCK
    upper = lax.broadcasted_iota(jnp.int32, (2 * groups, rows), 0) < groups
    even = lax.rem(lax.axis_index("ctx"), 2) == 0
    for slot, (back, odd_back) in enumerate(backs):
        if back != odd_back:
            back = jnp.where(even, back, odd_back)
        kpos = first - back * rows + lax.broadcasted_iota(jnp.int32, (rows, rows), 0)
        keep = kpos >= start[:1]
        if slot == 0:
            keep = keep & (kpos <= qpos[:1])
        table[slot, :rows, :] = jnp.where(keep, 0.0, LOW)
        line = jnp.ones((2 * groups, rows), jnp.float32)
        for piece in range(pieces):
            block = jnp.maximum(first // SCALE_BLOCK - back * pieces + piece, 0)
            column = jnp.sum(jnp.where(place == block, both, 0.0), axis=1, keepdims=True)
            wide = jnp.broadcast_to(column, (2 * groups, rows))
            at = rows + 2 * groups * piece
            table[slot, at : at + 2 * groups, :] = jnp.where(
                upper, wide * (math.log2(math.e) / math.sqrt(HEAD)), jnp.log2(wide)
            )
            line = jnp.where(lane == piece, wide, line)
        at = rows + 2 * groups * pieces
        table[slot, at : at + 2 * groups, :] = 1.0 / line
    copies[2].wait()
    copies[3].wait()


def setup(docs, scales, queries, own, groups, backs):
    rows = queries.shape[0]
    depth = rows + 2 * groups * (rows // SCALE_BLOCK + 1)
    scales = scales.transpose(1, 2, 0)
    far = [pltpu.with_memory_space_constraint(x, pltpu.HBM) for x in (docs, scales, queries)]
    return pl.pallas_call(
        functools.partial(setup_kernel, groups=groups, rows=rows, backs=backs),
        in_specs=[pl.BlockSpec(memory_space=pltpu.HBM)] * 3 + [pl.BlockSpec(memory_space=pltpu.VMEM)],
        out_specs=[pl.BlockSpec(memory_space=pltpu.VMEM)] * 3,
        out_shape=[
            pltpu.VMEM((len(backs), depth, rows), jnp.float32),
            pltpu.VMEM(queries.shape, queries.dtype),
            pltpu.VMEM(own.shape, own.dtype),
        ],
        scratch_shapes=[
            pltpu.SMEM(docs.shape, docs.dtype),
            pltpu.VMEM(scales.shape, scales.dtype),
            pltpu.SemaphoreType.DMA((4,)),
        ],
        compiler_params=pltpu.CompilerParams(vmem_limit_bytes=4 * 2**20),
    )(*far, own)


def kernel(*refs, slots, groups, rows, state, final, chunk):
    count = len(slots)
    refs = list(refs)
    sources = refs[: 2 + count + 2 * state]
    refs = refs[len(sources) :]
    if final:
        out = refs[0]
        refs = refs[1:]
    else:
        acc_out, stat_out = refs[:2]
        refs = refs[2:]
    buffers = sources
    bias, kparts, vparts, scores, probs = refs[:5]
    if final:
        stage, out_sems = refs[5:]
    width = sources[1].shape[1]
    heads = width // HEAD
    per = heads // groups
    pieces = rows // SCALE_BLOCK

    table, queries, blocks = buffers[0], buffers[1], buffers[2 : 2 + count]
    if state:
        acc_in, stat_in = buffers[2 + count], buffers[3 + count]

    deep = lax.broadcasted_iota(jnp.int32, (EXTRA, rows), 0)

    def prepare(group):
        at = group % 3
        for slot in range(count):
            for piece in range(pieces):
                source = pl.ds(piece * SCALE_BLOCK, SCALE_BLOCK)
                target = pl.ds(slot * rows + piece * SCALE_BLOCK, SCALE_BLOCK)
                base = rows + 2 * groups * piece + group
                bias[at, target, :] = table[slots[slot], source, :] + table[slots[slot], base + groups : base + groups + 1, :]
            base = rows + 2 * groups * pieces + groups + group
            inverse = table[slots[slot], base : base + 1, :]
            high = inverse.astype(jnp.bfloat16).astype(jnp.float32)
            ones = jnp.where(deep == 0, high, jnp.where(deep == 1, inverse - high, 0.0))
            columns = pl.ds(slot * rows, rows)
            kparts[at, columns, :] = blocks[slot][:, group * HEAD : (group + 1) * HEAD]
            vparts[at, :HEAD, columns] = blocks[slot][:, (groups + group) * HEAD : (groups + group + 1) * HEAD].T
            vparts[at, HEAD:, columns] = ones.astype(jnp.bfloat16)

    steps = heads // chunk
    tops = {}

    def some(step):
        return range(step * chunk, (step + 1) * chunk)

    def across(ref, offset, step):
        return jnp.concatenate([ref[offset + h : offset + h + 1, :] for h in some(step)], axis=1)

    def score_part(step):
        group = step * chunk // per
        if step * chunk % per == 0:
            prepare(group)
        query = jnp.concatenate([queries[:, h * HEAD : (h + 1) * HEAD] for h in some(step)], axis=0)
        score = lax.dot_general(kparts[group % 3], query, LAST, preferred_element_type=jnp.float32)
        scaled = []
        for at in range(count * pieces):
            base = rows + 2 * groups * (at % pieces) + group
            kscale = jnp.concatenate([table[slots[at // pieces], base : base + 1, :]] * chunk, axis=1)
            keys = slice(at * SCALE_BLOCK, (at + 1) * SCALE_BLOCK)
            scaled.append(score[keys] * kscale + jnp.concatenate([bias[group % 3, keys, :]] * chunk, axis=1))
        score = jnp.concatenate(scaled, axis=0)
        scores[step % 2] = score
        top = jnp.max(score, axis=0, keepdims=True)
        if state:
            top = jnp.maximum(top, across(stat_in, 0, step))
        tops[step] = top

    def prob_part(step):
        probs[step % 2] = jnp.exp2(scores[step % 2] - tops[step]).astype(jnp.bfloat16)

    def send(group):
        columns = pl.ds(group * per * HEAD, per * HEAD)
        return pltpu.make_async_copy(stage.at[:, columns], out.at[:, columns], out_sems.at[group])

    def value_part(step):
        group = step * chunk // per
        both = jnp.dot(vparts[group % 3], probs[step % 2], preferred_element_type=jnp.float32)
        total = both[HEAD : HEAD + 1] + both[HEAD + 1 : HEAD + 2]
        result = both[:HEAD]
        if state:
            keep = jnp.exp2(across(stat_in, 0, step) - tops[step])
            total = total + keep * across(stat_in, heads, step)
            old = jnp.concatenate([acc_in[h * HEAD : (h + 1) * HEAD, :] for h in some(step)], axis=1)
            result = result + keep * old
        if final:
            result = result * (1.0 / total)
        for at, h in enumerate(some(step)):
            lanes = slice(at * rows, (at + 1) * rows)
            if final:
                stage[:, h * HEAD : (h + 1) * HEAD] = result[:, lanes].astype(jnp.bfloat16).T
            else:
                acc_out[h * HEAD : (h + 1) * HEAD, :] = result[:, lanes]
                stat_out[h : h + 1, :] = tops[step][:, lanes]
                stat_out[heads + h : heads + h + 1, :] = total[:, lanes]
        if final and (step + 1) * chunk % per == 0:
            send(group).start()

    for step in range(steps + 2):
        if step < steps:
            score_part(step)
        if 1 <= step <= steps:
            prob_part(step - 1)
        if 2 <= step:
            value_part(step - 2)
    if final:
        for group in range(groups):
            send(group).wait()


def attend(table, queries, blocks, groups, slots, state=None, final=True, chunk=CHUNK):
    rows, width = queries.shape
    count = len(slots)
    span = count * rows
    heads = width // HEAD
    anywhere = pl.BlockSpec(memory_space=pl.ANY)
    state_shapes = [
        jax.ShapeDtypeStruct((width, rows), jnp.float32),
        jax.ShapeDtypeStruct((2 * heads, rows), jnp.float32),
    ]
    held = state is not None
    scratch = []
    scratch += [
        pltpu.VMEM((3, span, rows), jnp.float32),
        pltpu.VMEM((3, span, HEAD), jnp.bfloat16),
        pltpu.VMEM((3, HEAD + EXTRA, span), jnp.bfloat16),
        pltpu.VMEM((2, span, chunk * rows), jnp.float32),
        pltpu.VMEM((2, span, chunk * rows), jnp.bfloat16),
    ]
    if final:
        scratch += [pltpu.VMEM((rows, width), jnp.bfloat16), pltpu.SemaphoreType.DMA((groups,))]
    return pl.pallas_call(
        functools.partial(kernel, slots=slots, groups=groups, rows=rows, state=held, final=final, chunk=chunk),
        in_specs=[pl.BlockSpec(memory_space=pltpu.VMEM)] * (2 + count + 2 * held),
        out_specs=anywhere if final else [pl.BlockSpec(memory_space=pltpu.VMEM)] * 2,
        out_shape=jax.ShapeDtypeStruct((rows, width), jnp.bfloat16) if final else state_shapes,
        scratch_shapes=scratch,
        compiler_params=pltpu.CompilerParams(vmem_limit_bytes=24 * 2**20),
        cost_estimate=pl.CostEstimate(
            flops=4 * rows * width * span, bytes_accessed=4 * rows * width, transcendentals=heads * rows * span
        ),
    )(table, queries, *blocks, *(state if held else ()))


def ahead(block, distance):
    size = lax.axis_size("ctx")
    return lax.ppermute(block, "ctx", [(i, i + distance) for i in range(size - distance)])


def in_row(block, places):
    size = lax.axis_size("ctx")
    return lax.ppermute(block, "ctx", [(i, i // ROW * ROW + places[i % ROW]) for i in range(size)])


def per_device(queries, keys, values, key_value_scales, doc_lengths):
    groups = key_value_scales.shape[2]
    own = join(keys, values)
    fourth = ahead(own, 4)
    backs = ((0, 0), (4, 4), (2, 2), (3, 1), (1, 3))
    table, near, again = setup(doc_lengths, key_value_scales, queries, own, groups, backs)
    second = ahead(again, 2)
    inner, outer = pick(own, fourth)
    inner = in_row(inner, (1, 0, 3, 2))
    outer = in_row(outer, (3, 2, 1, 0))
    state = attend(table, near, (own, fourth, second), groups, (0, 1, 2), final=False)
    state = attend(table, near, (inner,), groups, (3,), state=state, final=False)
    return attend(table, near, (outer,), groups, (4,), state=state)


def solution(mesh):
    return jax.shard_map(
        per_device,
        mesh=mesh,
        in_specs=(
            P(("seq", "ctx"), None),
            P(("seq", "ctx"), None),
            P(("seq", "ctx"), None),
            P("seq", None, None),
            P("seq"),
        ),
        out_specs=P(("seq", "ctx"), None),
        check_vma=False,
    )
```

```python
import functools
import math

import jax
import jax.numpy as jnp
from jax import lax
from jax.experimental import pallas as pl
from jax.experimental.pallas import tpu as pltpu
from jax.sharding import PartitionSpec as P

SCALE_BLOCK = 32
HEAD = 128
LOW = -1e30
LAST = (((1,), (1,)), ((), ()))
EXTRA = 16
CHUNK = 8
QUERY_COPIES = 4
ROW = 4


def join_kernel(keys, values, own, sems):
    half = keys.shape[1]
    copies = [
        pltpu.make_async_copy(source, own.at[:, pl.ds(at * half, half)], sems.at[at])
        for at, source in enumerate((keys, values))
    ]
    for copy in copies:
        copy.start()
    for copy in copies:
        copy.wait()


def join(keys, values):
    rows, half = keys.shape
    far = [pltpu.with_memory_space_constraint(x, pltpu.HBM) for x in (keys, values)]
    return pl.pallas_call(
        join_kernel,
        in_specs=[pl.BlockSpec(memory_space=pltpu.HBM)] * 2,
        out_specs=pl.BlockSpec(memory_space=pltpu.VMEM),
        out_shape=pltpu.VMEM((rows, 2 * half), keys.dtype),
        scratch_shapes=[pltpu.SemaphoreType.DMA((2,))],
        compiler_params=pltpu.CompilerParams(vmem_limit_bytes=4 * 2**20),
    )(*far)


def pick_kernel(own, far, inner, outer):
    column = lax.rem(lax.axis_index("ctx"), ROW)
    mine, other = own[...], far[...]
    inner[...] = jnp.where(lax.rem(column, 2) == 0, mine, other)
    outer[...] = jnp.where(column < 2, mine, other)


def pick(own, far):
    vmem = pl.BlockSpec(memory_space=pltpu.VMEM)
    return pl.pallas_call(
        pick_kernel,
        in_specs=[vmem] * 2,
        out_specs=[vmem] * 2,
        out_shape=[pltpu.VMEM(own.shape, own.dtype)] * 2,
        compiler_params=pltpu.CompilerParams(vmem_limit_bytes=4 * 2**20),
    )(own, far)


def setup_kernel(docs_far, scales_far, queries, table, near, docs, scales, sems, *, groups, rows, backs):
    part = rows // QUERY_COPIES
    strips = [pl.ds(at * part, part) for at in range(QUERY_COPIES)]
    pairs = [(docs_far, docs), (scales_far, scales)] + [(queries.at[strip], near.at[strip]) for strip in strips]
    copies = [pltpu.make_async_copy(source, target, sems.at[at]) for at, (source, target) in enumerate(pairs)]
    for copy in copies:
        copy.start()
    copies[0].wait()
    copies[1].wait()
    first = lax.axis_index("ctx") * rows
    pieces = rows // SCALE_BLOCK
    qpos = first + lax.broadcasted_iota(jnp.int32, (8, rows), 1)

    def visit(doc, carry):
        end, start = carry
        end = end + docs[doc]
        return end, jnp.where(end <= qpos, end, start)

    _, start = lax.fori_loop(0, docs.shape[0], visit, (0, jnp.zeros((8, rows), jnp.int32)), unroll=8)
    both = jnp.concatenate([scales[0], scales[1]], axis=0)
    place = lax.broadcasted_iota(jnp.int32, both.shape, 1)
    lane = lax.broadcasted_iota(jnp.int32, (2 * groups, rows), 1) // SCALE_BLOCK
    upper = lax.broadcasted_iota(jnp.int32, (2 * groups, rows), 0) < groups
    even = lax.rem(lax.axis_index("ctx"), 2) == 0
    for slot, (back, odd_back) in enumerate(backs):
        if back != odd_back:
            back = jnp.where(even, back, odd_back)
        kpos = first - back * rows + lax.broadcasted_iota(jnp.int32, (rows, rows), 0)
        keep = kpos >= start[:1]
        if slot == 0:
            keep = keep & (kpos <= qpos[:1])
        table[slot, :rows, :] = jnp.where(keep, 0.0, LOW)
        line = jnp.ones((2 * groups, rows), jnp.float32)
        for piece in range(pieces):
            block = jnp.maximum(first // SCALE_BLOCK - back * pieces + piece, 0)
            column = jnp.sum(jnp.where(place == block, both, 0.0), axis=1, keepdims=True)
            wide = jnp.broadcast_to(column, (2 * groups, rows))
            at = rows + 2 * groups * piece
            table[slot, at : at + 2 * groups, :] = jnp.where(
                upper, wide * (math.log2(math.e) / math.sqrt(HEAD)), jnp.log2(wide)
            )
            line = jnp.where(lane == piece, wide, line)
        at = rows + 2 * groups * pieces
        table[slot, at : at + 2 * groups, :] = 1.0 / line
    for copy in copies[2:]:
        copy.wait()


def setup(docs, scales, queries, groups, backs):
    rows = queries.shape[0]
    depth = rows + 2 * groups * (rows // SCALE_BLOCK + 1)
    scales = scales.transpose(1, 2, 0)
    far = [pltpu.with_memory_space_constraint(x, pltpu.HBM) for x in (docs, scales, queries)]
    return pl.pallas_call(
        functools.partial(setup_kernel, groups=groups, rows=rows, backs=backs),
        in_specs=[pl.BlockSpec(memory_space=pltpu.HBM)] * 3,
        out_specs=[pl.BlockSpec(memory_space=pltpu.VMEM)] * 2,
        out_shape=[
            pltpu.VMEM((len(backs), depth, rows), jnp.float32),
            pltpu.VMEM(queries.shape, queries.dtype),
        ],
        scratch_shapes=[
            pltpu.SMEM(docs.shape, docs.dtype),
            pltpu.VMEM(scales.shape, scales.dtype),
            pltpu.SemaphoreType.DMA((2 + QUERY_COPIES,)),
        ],
        compiler_params=pltpu.CompilerParams(vmem_limit_bytes=4 * 2**20),
    )(*far)


def kernel(*refs, slots, groups, rows, state, final, chunk):
    count = len(slots)
    refs = list(refs)
    sources = refs[: 2 + count + 2 * state]
    refs = refs[len(sources) :]
    if final:
        out = refs[0]
        refs = refs[1:]
    else:
        acc_out, stat_out = refs[:2]
        refs = refs[2:]
    buffers = sources
    bias, kparts, vparts, scores, probs = refs[:5]
    if final:
        stage, out_sems = refs[5:]
    width = sources[1].shape[1]
    heads = width // HEAD
    per = heads // groups
    pieces = rows // SCALE_BLOCK

    table, queries, blocks = buffers[0], buffers[1], buffers[2 : 2 + count]
    if state:
        acc_in, stat_in = buffers[2 + count], buffers[3 + count]

    deep = lax.broadcasted_iota(jnp.int32, (EXTRA, rows), 0)

    def prepare(group):
        at = group % 3
        for slot in range(count):
            for piece in range(pieces):
                source = pl.ds(piece * SCALE_BLOCK, SCALE_BLOCK)
                target = pl.ds(slot * rows + piece * SCALE_BLOCK, SCALE_BLOCK)
                base = rows + 2 * groups * piece + group
                bias[at, target, :] = table[slots[slot], source, :] + table[slots[slot], base + groups : base + groups + 1, :]
            base = rows + 2 * groups * pieces + groups + group
            inverse = table[slots[slot], base : base + 1, :]
            high = inverse.astype(jnp.bfloat16).astype(jnp.float32)
            ones = jnp.where(deep == 0, high, jnp.where(deep == 1, inverse - high, 0.0))
            columns = pl.ds(slot * rows, rows)
            kparts[at, columns, :] = blocks[slot][:, group * HEAD : (group + 1) * HEAD]
            vparts[at, :HEAD, columns] = blocks[slot][:, (groups + group) * HEAD : (groups + group + 1) * HEAD].T
            vparts[at, HEAD:, columns] = ones.astype(jnp.bfloat16)

    steps = heads // chunk
    tops = {}

    def some(step):
        return range(step * chunk, (step + 1) * chunk)

    def across(ref, offset, step):
        return jnp.concatenate([ref[offset + h : offset + h + 1, :] for h in some(step)], axis=1)

    def score_part(step):
        group = step * chunk // per
        if step * chunk % per == 0:
            prepare(group)
        query = jnp.concatenate([queries[:, h * HEAD : (h + 1) * HEAD] for h in some(step)], axis=0)
        score = lax.dot_general(kparts[group % 3], query, LAST, preferred_element_type=jnp.float32)
        scaled = []
        for at in range(count * pieces):
            base = rows + 2 * groups * (at % pieces) + group
            kscale = jnp.concatenate([table[slots[at // pieces], base : base + 1, :]] * chunk, axis=1)
            keys = slice(at * SCALE_BLOCK, (at + 1) * SCALE_BLOCK)
            scaled.append(score[keys] * kscale + jnp.concatenate([bias[group % 3, keys, :]] * chunk, axis=1))
        score = jnp.concatenate(scaled, axis=0)
        scores[step % 2] = score
        top = jnp.max(score, axis=0, keepdims=True)
        if state:
            top = jnp.maximum(top, across(stat_in, 0, step))
        tops[step] = top

    def prob_part(step):
        probs[step % 2] = jnp.exp2(scores[step % 2] - tops[step]).astype(jnp.bfloat16)

    def send(group):
        columns = pl.ds(group * per * HEAD, per * HEAD)
        return pltpu.make_async_copy(stage.at[:, columns], out.at[:, columns], out_sems.at[group])

    def value_part(step):
        group = step * chunk // per
        both = jnp.dot(vparts[group % 3], probs[step % 2], preferred_element_type=jnp.float32)
        total = both[HEAD : HEAD + 1] + both[HEAD + 1 : HEAD + 2]
        result = both[:HEAD]
        if state:
            keep = jnp.exp2(across(stat_in, 0, step) - tops[step])
            total = total + keep * across(stat_in, heads, step)
            old = jnp.concatenate([acc_in[h * HEAD : (h + 1) * HEAD, :] for h in some(step)], axis=1)
            result = result + keep * old
        if final:
            result = result * (1.0 / total)
        for at, h in enumerate(some(step)):
            lanes = slice(at * rows, (at + 1) * rows)
            if final:
                stage[:, h * HEAD : (h + 1) * HEAD] = result[:, lanes].astype(jnp.bfloat16).T
            else:
                acc_out[h * HEAD : (h + 1) * HEAD, :] = result[:, lanes]
                stat_out[h : h + 1, :] = tops[step][:, lanes]
                stat_out[heads + h : heads + h + 1, :] = total[:, lanes]
        if final and (step + 1) * chunk % per == 0:
            send(group).start()

    for step in range(steps + 2):
        if step < steps:
            score_part(step)
        if 1 <= step <= steps:
            prob_part(step - 1)
        if 2 <= step:
            value_part(step - 2)
    if final:
        for group in range(groups):
            send(group).wait()


def attend(table, queries, blocks, groups, slots, state=None, final=True, chunk=CHUNK):
    rows, width = queries.shape
    count = len(slots)
    span = count * rows
    heads = width // HEAD
    anywhere = pl.BlockSpec(memory_space=pl.ANY)
    state_shapes = [
        jax.ShapeDtypeStruct((width, rows), jnp.float32),
        jax.ShapeDtypeStruct((2 * heads, rows), jnp.float32),
    ]
    held = state is not None
    scratch = []
    scratch += [
        pltpu.VMEM((3, span, rows), jnp.float32),
        pltpu.VMEM((3, span, HEAD), jnp.bfloat16),
        pltpu.VMEM((3, HEAD + EXTRA, span), jnp.bfloat16),
        pltpu.VMEM((2, span, chunk * rows), jnp.float32),
        pltpu.VMEM((2, span, chunk * rows), jnp.bfloat16),
    ]
    if final:
        scratch += [pltpu.VMEM((rows, width), jnp.bfloat16), pltpu.SemaphoreType.DMA((groups,))]
    return pl.pallas_call(
        functools.partial(kernel, slots=slots, groups=groups, rows=rows, state=held, final=final, chunk=chunk),
        in_specs=[pl.BlockSpec(memory_space=pltpu.VMEM)] * (2 + count + 2 * held),
        out_specs=anywhere if final else [pl.BlockSpec(memory_space=pltpu.VMEM)] * 2,
        out_shape=jax.ShapeDtypeStruct((rows, width), jnp.bfloat16) if final else state_shapes,
        scratch_shapes=scratch,
        compiler_params=pltpu.CompilerParams(vmem_limit_bytes=24 * 2**20),
        cost_estimate=pl.CostEstimate(
            flops=4 * rows * width * span, bytes_accessed=4 * rows * width, transcendentals=heads * rows * span
        ),
    )(table, queries, *blocks, *(state if held else ()))


def ahead(block, distance):
    size = lax.axis_size("ctx")
    return lax.ppermute(block, "ctx", [(i, i + distance) for i in range(size - distance)])


def in_row(block, places):
    size = lax.axis_size("ctx")
    return lax.ppermute(block, "ctx", [(i, i // ROW * ROW + places[i % ROW]) for i in range(size)])


def per_device(queries, keys, values, key_value_scales, doc_lengths):
    groups = key_value_scales.shape[2]
    own = join(keys, values)
    fourth = ahead(own, 4)
    second = ahead(own, 2)
    inner, outer = pick(own, fourth)
    inner = in_row(inner, (1, 0, 3, 2))
    outer = in_row(outer, (3, 2, 1, 0))
    backs = ((0, 0), (4, 4), (2, 2), (3, 1), (1, 3))
    table, near = setup(doc_lengths, key_value_scales, queries, groups, backs)
    state = attend(table, near, (own, fourth, second), groups, (0, 1, 2), final=False)
    state = attend(table, near, (inner,), groups, (3,), state=state, final=False)
    return attend(table, near, (outer,), groups, (4,), state=state)


def solution(mesh):
    return jax.shard_map(
        per_device,
        mesh=mesh,
        in_specs=(
            P(("seq", "ctx"), None),
            P(("seq", "ctx"), None),
            P(("seq", "ctx"), None),
            P("seq", None, None),
            P("seq"),
        ),
        out_specs=P(("seq", "ctx"), None),
        check_vma=False,
    )
```

```python
import functools
import math

import jax
import jax.numpy as jnp
from jax import lax
from jax.experimental import pallas as pl
from jax.experimental.pallas import tpu as pltpu
from jax.sharding import PartitionSpec as P

SCALE_BLOCK = 32
HEAD = 128
LOW = -1e30
LAST = (((1,), (1,)), ((), ()))
EXTRA = 16
CHUNK = 8
QUERY_COPIES = 4
ROW = 4


def join_kernel(keys, values, own, sems):
    half = keys.shape[1]
    copies = [
        pltpu.make_async_copy(source, own.at[:, pl.ds(at * half, half)], sems.at[at])
        for at, source in enumerate((keys, values))
    ]
    for copy in copies:
        copy.start()
    for copy in copies:
        copy.wait()


def join(keys, values):
    rows, half = keys.shape
    far = [pltpu.with_memory_space_constraint(x, pltpu.HBM) for x in (keys, values)]
    return pl.pallas_call(
        join_kernel,
        in_specs=[pl.BlockSpec(memory_space=pltpu.HBM)] * 2,
        out_specs=pl.BlockSpec(memory_space=pltpu.VMEM),
        out_shape=pltpu.VMEM((rows, 2 * half), keys.dtype),
        scratch_shapes=[pltpu.SemaphoreType.DMA((2,))],
        compiler_params=pltpu.CompilerParams(vmem_limit_bytes=4 * 2**20),
    )(*far)


def pick_kernel(own, far, inner, outer):
    column = lax.rem(lax.axis_index("ctx"), ROW)
    mine, other = own[...], far[...]
    inner[...] = jnp.where(lax.rem(column, 2) == 0, mine, other)
    outer[...] = jnp.where(column < 2, mine, other)


def pick(own, far):
    vmem = pl.BlockSpec(memory_space=pltpu.VMEM)
    return pl.pallas_call(
        pick_kernel,
        in_specs=[vmem] * 2,
        out_specs=[vmem] * 2,
        out_shape=[pltpu.VMEM(own.shape, own.dtype)] * 2,
        compiler_params=pltpu.CompilerParams(vmem_limit_bytes=4 * 2**20),
    )(own, far)


def setup_kernel(docs_far, scales_far, queries, table, near, docs, scales, sems, *, groups, rows, backs):
    part = rows // QUERY_COPIES
    strips = [pl.ds(at * part, part) for at in range(QUERY_COPIES)]
    pairs = [(docs_far, docs), (scales_far, scales)] + [(queries.at[strip], near.at[strip]) for strip in strips]
    copies = [pltpu.make_async_copy(source, target, sems.at[at]) for at, (source, target) in enumerate(pairs)]
    for copy in copies:
        copy.start()
    copies[0].wait()
    copies[1].wait()
    first = lax.axis_index("ctx") * rows
    pieces = rows // SCALE_BLOCK
    qpos = first + lax.broadcasted_iota(jnp.int32, (8, rows), 1)

    def visit(doc, carry):
        end, start = carry
        end = end + docs[doc]
        return end, jnp.where(end <= qpos, end, start)

    _, start = lax.fori_loop(0, docs.shape[0], visit, (0, jnp.zeros((8, rows), jnp.int32)), unroll=True)
    both = jnp.concatenate([scales[0], scales[1]], axis=0)
    place = lax.broadcasted_iota(jnp.int32, both.shape, 1)
    lane = lax.broadcasted_iota(jnp.int32, (2 * groups, rows), 1) // SCALE_BLOCK
    upper = lax.broadcasted_iota(jnp.int32, (2 * groups, rows), 0) < groups
    even = lax.rem(lax.axis_index("ctx"), 2) == 0
    for slot, (back, odd_back) in enumerate(backs):
        if back != odd_back:
            back = jnp.where(even, back, odd_back)
        kpos = first - back * rows + lax.broadcasted_iota(jnp.int32, (rows, rows), 0)
        keep = kpos >= start[:1]
        if slot == 0:
            keep = keep & (kpos <= qpos[:1])
        table[slot, :rows, :] = jnp.where(keep, 0.0, LOW)
        line = jnp.ones((2 * groups, rows), jnp.float32)
        for piece in range(pieces):
            block = jnp.maximum(first // SCALE_BLOCK - back * pieces + piece, 0)
            column = jnp.sum(jnp.where(place == block, both, 0.0), axis=1, keepdims=True)
            wide = jnp.broadcast_to(column, (2 * groups, rows))
            at = rows + 2 * groups * piece
            table[slot, at : at + 2 * groups, :] = jnp.where(
                upper, wide * (math.log2(math.e) / math.sqrt(HEAD)), jnp.log2(wide)
            )
            line = jnp.where(lane == piece, wide, line)
        at = rows + 2 * groups * pieces
        table[slot, at : at + 2 * groups, :] = 1.0 / line
    for copy in copies[2:]:
        copy.wait()


def setup(docs, scales, queries, groups, backs):
    rows = queries.shape[0]
    depth = rows + 2 * groups * (rows // SCALE_BLOCK + 1)
    scales = scales.transpose(1, 2, 0)
    far = [pltpu.with_memory_space_constraint(x, pltpu.HBM) for x in (docs, scales, queries)]
    return pl.pallas_call(
        functools.partial(setup_kernel, groups=groups, rows=rows, backs=backs),
        in_specs=[pl.BlockSpec(memory_space=pltpu.HBM)] * 3,
        out_specs=[pl.BlockSpec(memory_space=pltpu.VMEM)] * 2,
        out_shape=[
            pltpu.VMEM((len(backs), depth, rows), jnp.float32),
            pltpu.VMEM(queries.shape, queries.dtype),
        ],
        scratch_shapes=[
            pltpu.SMEM(docs.shape, docs.dtype),
            pltpu.VMEM(scales.shape, scales.dtype),
            pltpu.SemaphoreType.DMA((2 + QUERY_COPIES,)),
        ],
        compiler_params=pltpu.CompilerParams(vmem_limit_bytes=4 * 2**20),
    )(*far)


def kernel(*refs, slots, groups, rows, state, final, chunk):
    count = len(slots)
    refs = list(refs)
    sources = refs[: 2 + count + 2 * state]
    refs = refs[len(sources) :]
    if final:
        out = refs[0]
        refs = refs[1:]
    else:
        acc_out, stat_out = refs[:2]
        refs = refs[2:]
    buffers = sources
    bias, kparts, vparts, scores, probs = refs[:5]
    if final:
        stage, out_sems = refs[5:]
    width = sources[1].shape[1]
    heads = width // HEAD
    per = heads // groups
    pieces = rows // SCALE_BLOCK

    table, queries, blocks = buffers[0], buffers[1], buffers[2 : 2 + count]
    if state:
        acc_in, stat_in = buffers[2 + count], buffers[3 + count]

    deep = lax.broadcasted_iota(jnp.int32, (EXTRA, rows), 0)

    def prepare(group):
        at = group % 3
        for slot in range(count):
            for piece in range(pieces):
                source = pl.ds(piece * SCALE_BLOCK, SCALE_BLOCK)
                target = pl.ds(slot * rows + piece * SCALE_BLOCK, SCALE_BLOCK)
                base = rows + 2 * groups * piece + group
                bias[at, target, :] = table[slots[slot], source, :] + table[slots[slot], base + groups : base + groups + 1, :]
            base = rows + 2 * groups * pieces + groups + group
            inverse = table[slots[slot], base : base + 1, :]
            high = inverse.astype(jnp.bfloat16).astype(jnp.float32)
            ones = jnp.where(deep == 0, high, jnp.where(deep == 1, inverse - high, 0.0))
            columns = pl.ds(slot * rows, rows)
            kparts[at, columns, :] = blocks[slot][:, group * HEAD : (group + 1) * HEAD]
            vparts[at, :HEAD, columns] = blocks[slot][:, (groups + group) * HEAD : (groups + group + 1) * HEAD].T
            vparts[at, HEAD:, columns] = ones.astype(jnp.bfloat16)

    steps = heads // chunk
    tops = {}

    def some(step):
        return range(step * chunk, (step + 1) * chunk)

    def across(ref, offset, step):
        return jnp.concatenate([ref[offset + h : offset + h + 1, :] for h in some(step)], axis=1)

    def score_part(step):
        group = step * chunk // per
        if step * chunk % per == 0:
            prepare(group)
        query = jnp.concatenate([queries[:, h * HEAD : (h + 1) * HEAD] for h in some(step)], axis=0)
        score = lax.dot_general(kparts[group % 3], query, LAST, preferred_element_type=jnp.float32)
        scaled = []
        for at in range(count * pieces):
            base = rows + 2 * groups * (at % pieces) + group
            kscale = jnp.concatenate([table[slots[at // pieces], base : base + 1, :]] * chunk, axis=1)
            keys = slice(at * SCALE_BLOCK, (at + 1) * SCALE_BLOCK)
            scaled.append(score[keys] * kscale + jnp.concatenate([bias[group % 3, keys, :]] * chunk, axis=1))
        score = jnp.concatenate(scaled, axis=0)
        scores[step % 2] = score
        top = jnp.max(score, axis=0, keepdims=True)
        if state:
            top = jnp.maximum(top, across(stat_in, 0, step))
        tops[step] = top

    def prob_part(step):
        probs[step % 2] = jnp.exp2(scores[step % 2] - tops[step]).astype(jnp.bfloat16)

    def send(group):
        columns = pl.ds(group * per * HEAD, per * HEAD)
        return pltpu.make_async_copy(stage.at[:, columns], out.at[:, columns], out_sems.at[group])

    def value_part(step):
        group = step * chunk // per
        both = jnp.dot(vparts[group % 3], probs[step % 2], preferred_element_type=jnp.float32)
        total = both[HEAD : HEAD + 1] + both[HEAD + 1 : HEAD + 2]
        result = both[:HEAD]
        if state:
            keep = jnp.exp2(across(stat_in, 0, step) - tops[step])
            total = total + keep * across(stat_in, heads, step)
            old = jnp.concatenate([acc_in[h * HEAD : (h + 1) * HEAD, :] for h in some(step)], axis=1)
            result = result + keep * old
        if final:
            result = result * (1.0 / total)
        for at, h in enumerate(some(step)):
            lanes = slice(at * rows, (at + 1) * rows)
            if final:
                stage[:, h * HEAD : (h + 1) * HEAD] = result[:, lanes].astype(jnp.bfloat16).T
            else:
                acc_out[h * HEAD : (h + 1) * HEAD, :] = result[:, lanes]
                stat_out[h : h + 1, :] = tops[step][:, lanes]
                stat_out[heads + h : heads + h + 1, :] = total[:, lanes]
        if final and (step + 1) * chunk % per == 0:
            send(group).start()

    for step in range(steps + 2):
        if step < steps:
            score_part(step)
        if 1 <= step <= steps:
            prob_part(step - 1)
        if 2 <= step:
            value_part(step - 2)
    if final:
        for group in range(groups):
            send(group).wait()


def attend(table, queries, blocks, groups, slots, state=None, final=True, chunk=CHUNK):
    rows, width = queries.shape
    count = len(slots)
    span = count * rows
    heads = width // HEAD
    anywhere = pl.BlockSpec(memory_space=pl.ANY)
    state_shapes = [
        jax.ShapeDtypeStruct((width, rows), jnp.float32),
        jax.ShapeDtypeStruct((2 * heads, rows), jnp.float32),
    ]
    held = state is not None
    scratch = []
    scratch += [
        pltpu.VMEM((3, span, rows), jnp.float32),
        pltpu.VMEM((3, span, HEAD), jnp.bfloat16),
        pltpu.VMEM((3, HEAD + EXTRA, span), jnp.bfloat16),
        pltpu.VMEM((2, span, chunk * rows), jnp.float32),
        pltpu.VMEM((2, span, chunk * rows), jnp.bfloat16),
    ]
    if final:
        scratch += [pltpu.VMEM((rows, width), jnp.bfloat16), pltpu.SemaphoreType.DMA((groups,))]
    return pl.pallas_call(
        functools.partial(kernel, slots=slots, groups=groups, rows=rows, state=held, final=final, chunk=chunk),
        in_specs=[pl.BlockSpec(memory_space=pltpu.VMEM)] * (2 + count + 2 * held),
        out_specs=anywhere if final else [pl.BlockSpec(memory_space=pltpu.VMEM)] * 2,
        out_shape=jax.ShapeDtypeStruct((rows, width), jnp.bfloat16) if final else state_shapes,
        scratch_shapes=scratch,
        compiler_params=pltpu.CompilerParams(vmem_limit_bytes=24 * 2**20),
        cost_estimate=pl.CostEstimate(
            flops=4 * rows * width * span, bytes_accessed=4 * rows * width, transcendentals=heads * rows * span
        ),
    )(table, queries, *blocks, *(state if held else ()))


def ahead(block, distance):
    size = lax.axis_size("ctx")
    return lax.ppermute(block, "ctx", [(i, i + distance) for i in range(size - distance)])


def in_row(block, places):
    size = lax.axis_size("ctx")
    return lax.ppermute(block, "ctx", [(i, i // ROW * ROW + places[i % ROW]) for i in range(size)])


def per_device(queries, keys, values, key_value_scales, doc_lengths):
    groups = key_value_scales.shape[2]
    own = join(keys, values)
    fourth = ahead(own, 4)
    second = ahead(own, 2)
    inner, outer = pick(own, fourth)
    inner = in_row(inner, (1, 0, 3, 2))
    outer = in_row(outer, (3, 2, 1, 0))
    backs = ((0, 0), (4, 4), (2, 2), (3, 1), (1, 3))
    table, near = setup(doc_lengths, key_value_scales, queries, groups, backs)
    state = attend(table, near, (own, fourth, second), groups, (0, 1, 2), final=False)
    state = attend(table, near, (inner,), groups, (3,), state=state, final=False)
    return attend(table, near, (outer,), groups, (4,), state=state)


def solution(mesh):
    return jax.shard_map(
        per_device,
        mesh=mesh,
        in_specs=(
            P(("seq", "ctx"), None),
            P(("seq", "ctx"), None),
            P(("seq", "ctx"), None),
            P("seq", None, None),
            P("seq"),
        ),
        out_specs=P(("seq", "ctx"), None),
        check_vma=False,
    )
```
